256 devices in a mesh: row: 4 (over z_lo), col: 4 (over z_hi, core), seq: 16 (over x, y).
Axes of the slice: x: 4, y: 4, z: 8 (z_hi: 2, z_lo: 4; z = z_hi * 4 + z_lo), core: 2. Of those that a mesh axis runs over, the one named last changes fastest.
Arguments:
- states_a: int32 [8192, 1024], P('seq', 'row'), may hold values from 0 to 4
- states_b: int32 [8192, 1024], P('seq', 'col'), may hold values from 0 to 4
- field_a: float32 [5, 1024], P(None, 'row'), may hold values from -4 to 310
- field_b: float32 [5, 1024], P(None, 'col'), may hold values from -4 to 310
- couplings: float32 [5, 5, 1024, 1024], P(None, None, 'row', 'col'), may hold values from -0.2 to 0.2
- weights: float32 [8192], P('seq'), may hold values from 0.5 to 9
Outputs:
- new_couplings: float32 [5, 5, 1024, 1024], P(None, None, ('row', 'seq'), 'col')
The draws below stay inside these ranges and needn't reach their ends.
All inputs are finite; a program needn't handle non-finite values.
Results may differ from the reference program's by a relative error of at most 0.003.
Values may be sent and summed in bfloat16 or wider, within the bound.
No kernel may reach another device: no remote copies, remote signals or barrier semaphores. Data moves between devices by JAX's collectives and lax.ppermute only.
A program may use at most 64 MiB of HBM per device.

```python
import jax
import jax.numpy as jnp
from jax import lax

STATES = 5
LA = 1024
LB = 1024
GENOMES = 8192


def draw_field_a(key, part):
    key = jax.random.fold_in(key, 11)
    key_base = jax.random.fold_in(key, 0)
    base = jnp.clip(jax.random.normal(key_base, (STATES, LA), jnp.float32), -4.0, 4.0)
    return base


def draw_field_b(key, part):
    key = jax.random.fold_in(key, 12)
    key_base = jax.random.fold_in(key, 0)
    base = jnp.clip(jax.random.normal(key_base, (STATES, LB), jnp.float32), -4.0, 4.0)
    return base


def draw_weights(key, part):
    key = jax.random.fold_in(key, 13)
    ramp = jnp.arange(GENOMES, dtype=jnp.float32) / (GENOMES - 1)
    factor = jax.random.uniform(key, (GENOMES,), jnp.float32, 0.5, 1.0)
    return (1.0 + 2.0 * ramp) * factor


def set_ends(drawn, key, smallest, high):
    shape = drawn.shape
    spot = [jax.random.randint(jax.random.fold_in(key, axis), (), 0, shape[axis]) for axis in range(len(shape))]
    drawn = drawn.at[tuple(spot)].set(smallest)
    longest = shape.index(max(shape))
    spot[longest] = (spot[longest] + 1) % shape[longest]
    return drawn.at[tuple(spot)].set(high)


def block_scale(stream_key, shape, pieces, least, top_value):
    gain = 1.0
    for dim, parts in pieces:
        draws = jax.random.uniform(jax.random.fold_in(jax.random.fold_in(stream_key, 6), dim), (parts,), jnp.float32, least / len(pieces), top_value / len(pieces))
        gain = gain * jnp.repeat(jnp.exp(draws), shape[dim] // parts).reshape((-1,) + (1,) * (len(shape) - 1 - dim))
    return gain


def bell_draw(stream_key, extent, deviation, bound, pieces=(), kind=jnp.bfloat16):
    values = jax.random.normal(stream_key, extent, jnp.float32) * deviation
    if len(pieces) > 0:
        values = block_scale(stream_key, extent, pieces, -0.22, 0.18) * values
    return jnp.clip(values, min=-bound, max=bound).astype(kind)


def setup_inputs(seed: int = 0) -> dict:
    key_list = jax.random.split(jax.random.key(seed), 7)
    return {
        "states_a": set_ends(jax.random.randint(key_list[0], (GENOMES, LA), 0, STATES), jax.random.fold_in(key_list[0], 1), 0, STATES - 1).astype(jnp.int32),
        "states_b": set_ends(jax.random.randint(key_list[1], (GENOMES, LB), 0, STATES), jax.random.fold_in(key_list[1], 1), 0, STATES - 1).astype(jnp.int32),
        "field_a": draw_field_a(jax.random.fold_in(key_list[6], 71), 0),
        "field_b": draw_field_b(jax.random.fold_in(key_list[6], 71), 0),
        "couplings": bell_draw(key_list[4], (STATES, STATES, LA, LB), 0.03, 0.2, ((2, 4), (3, 4)), jnp.float32),
        "weights": draw_weights(jax.random.fold_in(key_list[6], 71), 0),
    }


step_scale = 64.0
ridge_weight = 0.002


def onehot(states):
    return (states[:, None, :] == jnp.arange(STATES, dtype=jnp.int32)[None, :, None]).astype(jnp.float32)


def residual(logits, onehot_rows, weights):
    top = jnp.max(logits, axis=1, keepdims=True)
    expo = jnp.exp(logits - top)
    prob = expo / jnp.sum(expo, axis=1, keepdims=True)
    return (weights[:, None, None] * (prob - onehot_rows)).astype(jnp.bfloat16)


def reference(states_a, states_b, field_a, field_b, couplings, weights):
    onehot_a = onehot(states_a)
    onehot_b = onehot(states_b)
    narrow = lax.optimization_barrier(couplings.astype(jnp.bfloat16)).astype(jnp.float32)
    logit_a = jnp.einsum("gbj,abij->gai", onehot_b, narrow) + field_a[None]
    logit_b = jnp.einsum("gai,abij->gbj", onehot_a, narrow) + field_b[None]
    resid_a = residual(logit_a, onehot_a, weights).astype(jnp.float32)
    resid_b = residual(logit_b, onehot_b, weights).astype(jnp.float32)
    grad_sum = jnp.einsum("gai,gbj->abij", resid_a, onehot_b) + jnp.einsum("gai,gbj->abij", onehot_a, resid_b)
    total = jnp.sum(weights)
    return (1.0 - step_scale * ridge_weight) * couplings - step_scale * grad_sum / total
```

```python
import functools

import jax
import jax.numpy as jnp
from jax import lax
from jax.experimental import pallas as pl
from jax.experimental.pallas import tpu as pltpu
from jax.sharding import PartitionSpec as P

STATES = 5
FREE = STATES - 1

step_scale = 64.0
ridge_weight = 0.002

OFFSET = 51.0 / 256.0
VMEM_LIMIT = 48 * 1024 * 1024

BF16 = jnp.bfloat16
F32 = jnp.float32


def params():
    return pltpu.CompilerParams(vmem_limit_bytes=VMEM_LIMIT)


def vmem():
    return pl.BlockSpec(memory_space=pltpu.VMEM)


def smem():
    return pl.BlockSpec(memory_space=pltpu.SMEM)


def partial_kernel(core_ref, sa_ref, sb_ref, j_ref, pb_ref, keep_ref, send_ref, hot_bt, acc_b, base_a):
    a = pl.program_id(0)
    n_loci_b = sb_ref.shape[1]
    chunks, _, rows, _ = pb_ref.shape
    half = keep_ref.shape[2]

    @pl.when(a == 0)
    def _():
        sbt = sb_ref[...].astype(F32).T
        for b in range(STATES):
            hot_bt[pl.ds(b * n_loci_b, n_loci_b), :] = jnp.where(sbt == float(b), 1.0, 0.0).astype(BF16)

    narrow = jnp.concatenate([j_ref[0, b].astype(BF16) for b in range(STATES)], axis=1)
    hot_a = jnp.where(sa_ref[...] == a, 1.0, 0.0).astype(BF16)
    part_b = jnp.dot(hot_a, narrow, preferred_element_type=F32)

    @pl.when(a == 0)
    def _():
        acc_b[...] = part_b

    @pl.when(a > 0)
    def _():
        acc_b[...] += part_b

    part_a = jnp.dot(narrow, hot_bt[...], preferred_element_type=F32)

    @pl.when(a == 0)
    def _():
        base_a[...] = part_a

    @pl.when(a > 0)
    def _():
        free = part_a - base_a[...]
        low, high = free[:, :half], free[:, half:]
        first = core_ref[0] == 0
        keep_ref[a - 1] = jnp.where(first, low, high).astype(BF16)
        send_ref[a - 1] = jnp.where(first, high, low).astype(BF16)

    @pl.when(a == STATES - 1)
    def _():
        for k in range(chunks):
            block = acc_b[pl.ds(k * rows, rows), :]
            zero = block[:, :n_loci_b]
            for b in range(1, STATES):
                pb_ref[k, b - 1] = (block[:, b * n_loci_b : (b + 1) * n_loci_b] - zero).astype(BF16)


def partial_logits(core, states_a, states_b, couplings, chunks):
    genomes, la = states_a.shape
    lb = states_b.shape[1]
    rows, half = genomes // chunks, genomes // 2
    whole = lambda *shape: pl.BlockSpec(shape, lambda a: (0,) * len(shape))
    return pl.pallas_call(
        partial_kernel,
        grid=(STATES,),
        in_specs=[
            smem(),
            whole(genomes, la),
            whole(genomes, lb),
            pl.BlockSpec((1, STATES, la, lb), lambda a: (a, 0, 0, 0)),
        ],
        out_specs=[whole(chunks, FREE, rows, lb), whole(FREE, la, half), whole(FREE, la, half)],
        out_shape=[
            jax.ShapeDtypeStruct((chunks, FREE, rows, lb), BF16),
            jax.ShapeDtypeStruct((FREE, la, half), BF16),
            jax.ShapeDtypeStruct((FREE, la, half), BF16),
        ],
        scratch_shapes=[
            pltpu.VMEM((STATES * lb, genomes), BF16),
            pltpu.VMEM((genomes, STATES * lb), F32),
            pltpu.VMEM((la, genomes), F32),
        ],
        compiler_params=params(),
        name="partial_logits",
    )(core, states_a, states_b, couplings)


def free_residuals(logits, states, weight, out_ref):
    top = jnp.maximum(jnp.maximum(logits[0], logits[1]), jnp.maximum(logits[2], logits[3]))
    top = jnp.maximum(top, 0.0)
    expo = [jnp.exp(x - top) for x in logits]
    scale = 1.0 / (expo[0] + expo[1] + expo[2] + expo[3] + jnp.exp(-top))
    for k in range(FREE):
        hot = jnp.where(states == k + 1, 1.0, 0.0)
        out_ref[k] = (weight * (expo[k] * scale - hot)).astype(BF16)


def residual_b_kernel(mine_ref, other_ref, field_ref, states_ref, weight_ref, out_ref):
    logits = [
        mine_ref[k].astype(F32) + other_ref[k].astype(F32) + (field_ref[k + 1 : k + 2, :] - field_ref[0:1, :])
        for k in range(FREE)
    ]
    free_residuals(logits, states_ref[...], weight_ref[...], out_ref)


def residual_b(mine, other, field_b, states_b, weight_column, chunk):
    free, rows, lb = mine.shape
    whole = lambda *shape: pl.BlockSpec(shape, lambda i: (0,) * len(shape))
    return pl.pallas_call(
        residual_b_kernel,
        grid=(1,),
        in_specs=[
            whole(free, rows, lb),
            whole(free, rows, lb),
            whole(STATES, lb),
            pl.BlockSpec((rows, lb), lambda i: (chunk, 0)),
            pl.BlockSpec((rows, 1), lambda i: (chunk, 0)),
        ],
        out_specs=whole(free, rows, lb),
        out_shape=jax.ShapeDtypeStruct((free, rows, lb), BF16),
        compiler_params=params(),
        name="residual_b",
    )(mine, other, field_b, states_b, weight_column)


def residual_a_kernel(core_ref, mine_ref, other_ref, field_ref, states_ref, weight_ref, out_ref):
    half = mine_ref.shape[2]
    start = pl.multiple_of(core_ref[0] * half, half)
    states = states_ref[pl.ds(start, half), :].astype(F32).T.astype(jnp.int32)
    weight = weight_ref[pl.ds(core_ref[0], 1), :]
    logits = [
        mine_ref[k].astype(F32) + other_ref[k].astype(F32) + (field_ref[:, k + 1 : k + 2] - field_ref[:, 0:1])
        for k in range(FREE)
    ]
    free_residuals(logits, states, weight, out_ref)


def residual_a(core, mine, other, field_column, states_a, weight_rows):
    return pl.pallas_call(
        residual_a_kernel,
        in_specs=[smem()] + [vmem()] * 5,
        out_specs=vmem(),
        out_shape=jax.ShapeDtypeStruct(mine.shape, BF16),
        compiler_params=params(),
        name="residual_a",
    )(core, mine, other, field_column, states_a, weight_rows)


def two_halves(x):
    high = x.astype(BF16)
    return high, (x - high.astype(F32)).astype(BF16)


def gradient_kernel(chunks, where_ref, ra_ref, ra_other_ref, *refs):
    rb_refs, rest = refs[: 2 * chunks], refs[2 * chunks :]
    sa_ref, sb_ref, weight_ref, out_ref = rest
    core, middle = where_ref[0], where_ref[1]
    half = ra_ref.shape[2]
    parts, _, rows, lb = out_ref.shape
    la = parts * rows
    first = core == 0

    sat = sa_ref[...].astype(F32).T
    sb = sb_ref[...]
    rights = []
    sums_b = []
    for b in range(FREE):
        hot = jnp.where(sb == b + 1, 1.0 - OFFSET, -OFFSET).astype(BF16)
        resid = [
            jnp.where(middle == 1, rb_refs[2 * k][b], rb_refs[2 * k + 1][b]) for k in range(chunks)
        ]
        sums_b.append(sum(jnp.sum(r.astype(F32), axis=0, keepdims=True) for r in resid))
        rights.append(jnp.concatenate([hot] + resid, axis=0))
    right = jnp.concatenate(rights, axis=1)
    lane = lax.broadcasted_iota(jnp.int32, (la, lb), 1)
    margin_a = jnp.zeros((la, lb), F32)
    for a in range(FREE):
        mine, other = ra_ref[a], ra_other_ref[a]
        low, high = jnp.where(first, mine, other), jnp.where(first, other, mine)
        hot = jnp.where(sat == float(a + 1), 1.0 - OFFSET, -OFFSET).astype(BF16)
        left = jnp.concatenate([low, high, hot], axis=1)
        grad = jnp.dot(left, right, preferred_element_type=F32).astype(BF16)
        for b in range(FREE):
            out_ref[:, a * FREE + b] = grad[:, b * lb : (b + 1) * lb].reshape(parts, rows, lb)
        sum_a = jnp.sum(low.astype(F32), axis=1, keepdims=True) + jnp.sum(high.astype(F32), axis=1, keepdims=True)
        big, small = two_halves(sum_a)
        margin_a = jnp.where(lane == a, big.astype(F32), margin_a)
        margin_a = jnp.where(lane == FREE + a, small.astype(F32), margin_a)
    out_ref[:, FREE * FREE] = margin_a.astype(BF16).reshape(parts, rows, lb)

    line = lax.broadcasted_iota(jnp.int32, (rows, lb), 0)
    margin_b = jnp.zeros((rows, lb), F32)
    weight_sum = jnp.sum(weight_ref[...], keepdims=True).reshape(1, 1)
    for k, value in enumerate(sums_b + [weight_sum]):
        big, small = two_halves(value)
        margin_b = jnp.where(line == 2 * k, big.astype(F32), margin_b)
        margin_b = jnp.where(line == 2 * k + 1, small.astype(F32), margin_b)
    out_ref[:, FREE * FREE + 1] = jnp.broadcast_to(margin_b.astype(BF16)[None], (parts, rows, lb))


def gradient_parts(where, resid_a, resid_a_other, resid_b_pairs, states_a, states_b, weight_rows, parts):
    la, lb = states_a.shape[1], states_b.shape[1]
    chunks = len(resid_b_pairs)
    flat = [x for pair in resid_b_pairs for x in pair]
    return pl.pallas_call(
        functools.partial(gradient_kernel, chunks),
        in_specs=[smem()] + [vmem()] * (2 + 2 * chunks + 3),
        out_specs=vmem(),
        out_shape=jax.ShapeDtypeStruct((parts, FREE * FREE + 2, la // parts, lb), BF16),
        compiler_params=params(),
        name="gradient_parts",
    )(where, resid_a, resid_a_other, *flat, states_a, states_b, weight_rows)


def update_kernel(where_ref, parts_ref, j_ref, out_ref):
    total = parts_ref[0].astype(F32)
    for k in range(1, parts_ref.shape[0]):
        total = total + parts_ref[k].astype(F32)
    margin_a, margin_b = total[FREE * FREE], total[FREE * FREE + 1]
    col = [margin_a[:, a : a + 1] + margin_a[:, FREE + a : FREE + a + 1] for a in range(FREE)]
    row = [margin_b[2 * b : 2 * b + 1, :] + margin_b[2 * b + 1 : 2 * b + 2, :] for b in range(FREE)]
    weight = margin_b[2 * FREE : 2 * FREE + 1, :] + margin_b[2 * FREE + 1 : 2 * FREE + 2, :]
    scale = step_scale / weight
    keep = 1.0 - step_scale * ridge_weight

    def emit(a, b, grad):
        out_ref[a, b] = keep * j_ref[a, b] - scale * grad

    along_b = [None] * FREE
    corner = None
    for a in range(FREE):
        along_a = None
        for b in range(FREE):
            grad = total[a * FREE + b] + OFFSET * (col[a] + row[b])
            emit(a + 1, b + 1, grad)
            along_a = grad if along_a is None else along_a + grad
            along_b[b] = grad if a == 0 else along_b[b] + grad
        edge = col[a] - along_a
        emit(a + 1, 0, edge)
        corner = edge if corner is None else corner + edge
    for b in range(FREE):
        emit(0, b + 1, row[b] - along_b[b])
    emit(0, 0, -(row[0] + row[1] + row[2] + row[3]) - corner)


def update(where, parts, couplings):
    count, comps, rows, lb = parts.shape
    return pl.pallas_call(
        update_kernel,
        grid_spec=pltpu.PrefetchScalarGridSpec(
            num_scalar_prefetch=1,
            grid=(1,),
            in_specs=[
                pl.BlockSpec((count, comps, rows, lb), lambda i, s: (0, 0, 0, 0)),
                pl.BlockSpec((STATES, STATES, rows, lb), lambda i, s: (0, 0, s[0], 0)),
            ],
            out_specs=pl.BlockSpec((STATES, STATES, rows, lb), lambda i, s: (0, 0, 0, 0)),
        ),
        out_shape=jax.ShapeDtypeStruct((STATES, STATES, rows, lb), F32),
        compiler_params=params(),
        name="update",
    )(where, parts, couplings)


CHUNKS = 2


def on_device(sizes, states_a, states_b, field_a, field_b, couplings, weights):
    seq = sizes["seq"]
    genomes = states_a.shape[0]
    row, col = lax.axis_index("row"), lax.axis_index("col")
    core = (col % 2).astype(jnp.int32)
    middle = jnp.logical_or(row == 1, row == 2).astype(jnp.int32)
    core_arg = core.reshape(1)
    weight_rows = weights.reshape(2, genomes // 2)
    weight_column = weights.reshape(genomes, 1)
    field_column = field_a.T

    part_b, keep, send = partial_logits(core_arg, states_a, states_b, couplings, CHUNKS)

    swap_core = [(c, c ^ 1) for c in range(4)]
    swap_far = [(c, c ^ 2) for c in range(4)]
    got = lax.ppermute(send, "col", swap_core)

    inward = [lax.ppermute(part_b[k], "row", [(0, 1), (3, 2)]) for k in range(CHUNKS)]

    both = (keep.astype(F32) + got.astype(F32)).astype(BF16)
    far = lax.ppermute(both, "col", swap_far)

    pairs = []
    for k in range(CHUNKS):
        near = (part_b[k].astype(F32) + inward[k].astype(F32)).astype(BF16)
        across = lax.ppermute(near, "row", [(1, 2), (2, 1)])
        resid = residual_b(near, across, field_b, states_b, weight_column, k)
        outward = lax.ppermute(resid, "row", [(1, 0), (2, 3)])
        pairs.append((resid, outward))

    resid_a = residual_a(core_arg, both, far, field_column, states_a, weight_rows)
    resid_a_other = lax.ppermute(resid_a, "col", swap_core)

    where = jnp.stack([core, middle])
    parts = gradient_parts(where, resid_a, resid_a_other, pairs, states_a, states_b, weight_rows, seq)
    got_parts = lax.all_to_all(parts, "seq", 0, 0)
    return update(lax.axis_index("seq").astype(jnp.int32).reshape(1), got_parts, couplings)


def solution(mesh):
    placed = (
        P("seq", "row"),
        P("seq", "col"),
        P(None, "row"),
        P(None, "col"),
        P(None, None, "row", "col"),
        P("seq"),
    )
    return jax.shard_map(
        functools.partial(on_device, dict(mesh.shape)),
        mesh=mesh,
        in_specs=placed,
        out_specs=P(None, None, ("row", "seq"), "col"),
        check_vma=False,
    )
```

```python
import functools

import jax
import jax.numpy as jnp
from jax import lax
from jax.experimental import pallas as pl
from jax.experimental.pallas import tpu as pltpu
from jax.sharding import PartitionSpec as P

STATES = 5
FREE = STATES - 1

step_scale = 64.0
ridge_weight = 0.002

OFFSET = 51.0 / 256.0
VMEM_LIMIT = 48 * 1024 * 1024

BF16 = jnp.bfloat16
F32 = jnp.float32


def params():
    return pltpu.CompilerParams(vmem_limit_bytes=VMEM_LIMIT)


def vmem():
    return pl.BlockSpec(memory_space=pltpu.VMEM)


def smem():
    return pl.BlockSpec(memory_space=pltpu.SMEM)


def center_hot(states, k):
    return jnp.where(states == k, 1.0 - OFFSET, -OFFSET).astype(BF16)


def narrow_row(j_ref):
    return jnp.concatenate([j_ref[0, b].astype(BF16) for b in range(STATES)], axis=1)


def add_logits_b(a, hot_a, narrow, acc_b, pb_ref):
    part_b = jnp.dot(hot_a, narrow, preferred_element_type=F32)
    width = pb_ref.shape[2]

    @pl.when(a == 0)
    def _():
        acc_b[...] = part_b

    @pl.when(a > 0)
    def _():
        acc_b[...] += part_b

    @pl.when(a == STATES - 1)
    def _():
        zero = acc_b[:, :width]
        for b in range(1, STATES):
            pb_ref[b - 1] = (acc_b[:, b * width : (b + 1) * width] - zero).astype(BF16)


def first_kernel(sa_ref, j_ref, pb_ref, acc_b):
    a = pl.program_id(0)
    hot_a = jnp.where(sa_ref[...] == a, 1.0, 0.0).astype(BF16)
    add_logits_b(a, hot_a, narrow_row(j_ref), acc_b, pb_ref)


def whole(*shape):
    return pl.BlockSpec(shape, lambda *_: (0,) * len(shape))


def first_logits(states_a, couplings):
    genomes, la = states_a.shape
    width = couplings.shape[3] // 2
    return pl.pallas_call(
        first_kernel,
        grid=(STATES,),
        in_specs=[whole(genomes, la), pl.BlockSpec((1, STATES, la, width), lambda a: (a, 0, 0, 0))],
        out_specs=whole(FREE, genomes, width),
        out_shape=jax.ShapeDtypeStruct((FREE, genomes, width), BF16),
        scratch_shapes=[pltpu.VMEM((genomes, STATES * width), F32)],
        compiler_params=params(),
        name="first_logits",
    )(states_a, couplings)


def second_kernel(core_ref, sa_ref, sb_ref, j_ref, pb_ref, keep_ref, send_ref, hot_bt, acc_b, base_a):
    a = pl.program_id(0)
    n_loci_b = sb_ref.shape[1]
    width = pb_ref.shape[2]
    half = keep_ref.shape[2]

    @pl.when(a == 0)
    def _():
        sbt = sb_ref[...].astype(F32).T
        for b in range(STATES):
            hot_bt[pl.ds(b * n_loci_b, n_loci_b), :] = jnp.where(sbt == float(b), 1.0, 0.0).astype(BF16)

    narrow = narrow_row(j_ref)
    hot_a = jnp.where(sa_ref[...] == a, 1.0, 0.0).astype(BF16)
    upper = [narrow[:, b * n_loci_b + width : (b + 1) * n_loci_b] for b in range(STATES)]
    add_logits_b(a, hot_a, jnp.concatenate(upper, axis=1), acc_b, pb_ref)

    part_a = jnp.dot(narrow, hot_bt[...], preferred_element_type=F32)

    @pl.when(a == 0)
    def _():
        base_a[...] = part_a

    @pl.when(a > 0)
    def _():
        free = part_a - base_a[...]
        low, high = free[:, :half], free[:, half:]
        first = core_ref[0] == 0
        keep_ref[a - 1] = jnp.where(first, low, high).astype(BF16)
        send_ref[a - 1] = jnp.where(first, high, low).astype(BF16)


def second_logits(core, states_a, states_b, couplings):
    genomes, la = states_a.shape
    lb = states_b.shape[1]
    width, half = lb // 2, genomes // 2
    return pl.pallas_call(
        second_kernel,
        grid=(STATES,),
        in_specs=[
            smem(),
            whole(genomes, la),
            whole(genomes, lb),
            pl.BlockSpec((1, STATES, la, lb), lambda a: (a, 0, 0, 0)),
        ],
        out_specs=[whole(FREE, genomes, width), whole(FREE, la, half), whole(FREE, la, half)],
        out_shape=[
            jax.ShapeDtypeStruct((FREE, genomes, width), BF16),
            jax.ShapeDtypeStruct((FREE, la, half), BF16),
            jax.ShapeDtypeStruct((FREE, la, half), BF16),
        ],
        scratch_shapes=[
            pltpu.VMEM((STATES * lb, genomes), BF16),
            pltpu.VMEM((genomes, STATES * width), F32),
            pltpu.VMEM((la, genomes), F32),
        ],
        compiler_params=params(),
        name="second_logits",
    )(core, states_a, states_b, couplings)


def free_residuals(logits, states, weight, out_ref):
    top = jnp.maximum(jnp.maximum(logits[0], logits[1]), jnp.maximum(logits[2], logits[3]))
    top = jnp.maximum(top, 0.0)
    expo = [jnp.exp(x - top) for x in logits]
    scale = 1.0 / (expo[0] + expo[1] + expo[2] + expo[3] + jnp.exp(-top))
    for k in range(FREE):
        hot = jnp.where(states == k + 1, 1.0, 0.0)
        out_ref[k] = (weight * (expo[k] * scale - hot)).astype(BF16)


def residual_b_kernel(mine_ref, other_ref, field_ref, states_ref, weight_ref, out_ref):
    logits = [
        mine_ref[k].astype(F32) + other_ref[k].astype(F32) + (field_ref[k + 1 : k + 2, :] - field_ref[0:1, :])
        for k in range(FREE)
    ]
    free_residuals(logits, states_ref[...], weight_ref[...], out_ref)


def residual_b(mine, other, field_b, states_b, weight_column, part):
    free, genomes, width = mine.shape
    return pl.pallas_call(
        residual_b_kernel,
        grid=(1,),
        in_specs=[
            whole(free, genomes, width),
            whole(free, genomes, width),
            pl.BlockSpec((STATES, width), lambda i: (0, part)),
            pl.BlockSpec((genomes, width), lambda i: (0, part)),
            whole(genomes, 1),
        ],
        out_specs=whole(free, genomes, width),
        out_shape=jax.ShapeDtypeStruct((free, genomes, width), BF16),
        compiler_params=params(),
        name="residual_b",
    )(mine, other, field_b, states_b, weight_column)


def residual_a_kernel(core_ref, mine_ref, other_ref, field_ref, states_ref, weight_ref, out_ref):
    half = mine_ref.shape[2]
    start = pl.multiple_of(core_ref[0] * half, half)
    states = states_ref[pl.ds(start, half), :].astype(F32).T.astype(jnp.int32)
    weight = weight_ref[pl.ds(core_ref[0], 1), :]
    logits = [
        mine_ref[k].astype(F32) + other_ref[k].astype(F32) + (field_ref[:, k + 1 : k + 2] - field_ref[:, 0:1])
        for k in range(FREE)
    ]
    free_residuals(logits, states, weight, out_ref)


def residual_a(core, mine, other, field_column, states_a, weight_rows):
    return pl.pallas_call(
        residual_a_kernel,
        in_specs=[smem()] + [vmem()] * 5,
        out_specs=vmem(),
        out_shape=jax.ShapeDtypeStruct(mine.shape, BF16),
        compiler_params=params(),
        name="residual_a",
    )(core, mine, other, field_column, states_a, weight_rows)


def two_halves(x):
    high = x.astype(BF16)
    return high, (x - high.astype(F32)).astype(BF16)


def gradient_kernel(part, where_ref, ra_ref, ra_other_ref, rb_ref, rb_other_ref, sa_ref, sb_ref, weight_ref, out_ref):
    core, middle = where_ref[0], where_ref[1]
    parts, _, rows, width = out_ref.shape
    la = parts * rows
    first = core == 0

    sat = sa_ref[...].astype(F32).T
    sb = sb_ref[...]
    rights = []
    sums_b = []
    for b in range(FREE):
        resid = jnp.where(middle == 1, rb_ref[b], rb_other_ref[b])
        sums_b.append(jnp.sum(resid.astype(F32), axis=0, keepdims=True))
        rights.append(jnp.concatenate([center_hot(sb, b + 1), resid], axis=0))
    right = jnp.concatenate(rights, axis=1)
    lane = lax.broadcasted_iota(jnp.int32, (la, width), 1)
    margin_a = jnp.zeros((la, width), F32)
    for a in range(FREE):
        mine, other = ra_ref[a], ra_other_ref[a]
        low, high = jnp.where(first, mine, other), jnp.where(first, other, mine)
        left = jnp.concatenate([low, high, center_hot(sat, float(a + 1))], axis=1)
        grad = jnp.dot(left, right, preferred_element_type=F32).astype(BF16)
        for b in range(FREE):
            out_ref[:, a * FREE + b] = grad[:, b * width : (b + 1) * width].reshape(parts, rows, width)
        if part == 0:
            sum_a = jnp.sum(low.astype(F32), axis=1, keepdims=True) + jnp.sum(high.astype(F32), axis=1, keepdims=True)
            big, small = two_halves(sum_a)
            margin_a = jnp.where(lane == a, big.astype(F32), margin_a)
            margin_a = jnp.where(lane == FREE + a, small.astype(F32), margin_a)

    line = lax.broadcasted_iota(jnp.int32, (rows, width), 0)
    margin_b = jnp.zeros((rows, width), F32)
    weight_sum = jnp.sum(weight_ref[...], keepdims=True).reshape(1, 1)
    for k, value in enumerate(sums_b + [weight_sum]):
        big, small = two_halves(value)
        margin_b = jnp.where(line == 2 * k, big.astype(F32), margin_b)
        margin_b = jnp.where(line == 2 * k + 1, small.astype(F32), margin_b)
    out_ref[:, FREE * FREE] = jnp.broadcast_to(margin_b.astype(BF16)[None], (parts, rows, width))
    if part == 0:
        out_ref[:, FREE * FREE + 1] = margin_a.astype(BF16).reshape(parts, rows, width)


def gradient_parts(where, resid_a, resid_a_other, resid_b, resid_b_other, states_a, states_b, weight_rows, parts, part):
    genomes, la = states_a.shape
    free, _, width = resid_b.shape
    comps = FREE * FREE + (2 if part == 0 else 1)
    return pl.pallas_call(
        functools.partial(gradient_kernel, part),
        grid=(1,),
        in_specs=[
            smem(),
            whole(*resid_a.shape),
            whole(*resid_a.shape),
            whole(*resid_b.shape),
            whole(*resid_b.shape),
            whole(genomes, la),
            pl.BlockSpec((genomes, width), lambda i: (0, part)),
            whole(*weight_rows.shape),
        ],
        out_specs=whole(parts, comps, la // parts, width),
        out_shape=jax.ShapeDtypeStruct((parts, comps, la // parts, width), BF16),
        compiler_params=params(),
        name="gradient_parts",
    )(where, resid_a, resid_a_other, resid_b, resid_b_other, states_a, states_b, weight_rows)


def update_kernel(where_ref, first_ref, second_ref, j_ref, out_ref):
    width = first_ref.shape[3]
    keep = 1.0 - step_scale * ridge_weight
    for part, parts_ref in enumerate((first_ref, second_ref)):
        total = parts_ref[0].astype(F32)
        for k in range(1, parts_ref.shape[0]):
            total = total + parts_ref[k].astype(F32)
        margin_b = total[FREE * FREE]
        if part == 0:
            margin_a = total[FREE * FREE + 1]
            col = [margin_a[:, a : a + 1] + margin_a[:, FREE + a : FREE + a + 1] for a in range(FREE)]
        row = [margin_b[2 * b : 2 * b + 1, :] + margin_b[2 * b + 1 : 2 * b + 2, :] for b in range(FREE)]
        weight = margin_b[2 * FREE : 2 * FREE + 1, :] + margin_b[2 * FREE + 1 : 2 * FREE + 2, :]
        scale = step_scale / weight
        lanes = pl.ds(part * width, width)

        def emit(a, b, grad):
            out_ref[a, b, :, lanes] = keep * j_ref[a, b, :, lanes] - scale * grad

        along_b = [None] * FREE
        corner = None
        for a in range(FREE):
            along_a = None
            for b in range(FREE):
                grad = total[a * FREE + b] + OFFSET * (col[a] + row[b])
                emit(a + 1, b + 1, grad)
                along_a = grad if along_a is None else along_a + grad
                along_b[b] = grad if a == 0 else along_b[b] + grad
            edge = col[a] - along_a
            emit(a + 1, 0, edge)
            corner = edge if corner is None else corner + edge
        for b in range(FREE):
            emit(0, b + 1, row[b] - along_b[b])
        emit(0, 0, -(row[0] + row[1] + row[2] + row[3]) - corner)


def update(where, parts, couplings):
    rows = parts[0].shape[2]
    lb = couplings.shape[3]
    return pl.pallas_call(
        update_kernel,
        grid_spec=pltpu.PrefetchScalarGridSpec(
            num_scalar_prefetch=1,
            grid=(1,),
            in_specs=[whole(*x.shape) for x in parts]
            + [pl.BlockSpec((STATES, STATES, rows, lb), lambda i, s: (0, 0, s[0], 0))],
            out_specs=whole(STATES, STATES, rows, lb),
        ),
        out_shape=jax.ShapeDtypeStruct((STATES, STATES, rows, lb), F32),
        compiler_params=params(),
        name="update",
    )(where, *parts, couplings)


def after(x, *others):
    return lax.optimization_barrier((x,) + others)[0]


def add(x, y):
    return (x.astype(F32) + y.astype(F32)).astype(BF16)


def on_device(sizes, states_a, states_b, field_a, field_b, couplings, weights):
    seq = sizes["seq"]
    genomes = states_a.shape[0]
    row, col = lax.axis_index("row"), lax.axis_index("col")
    core = (col % 2).astype(jnp.int32)
    middle = jnp.logical_or(row == 1, row == 2).astype(jnp.int32)
    where = jnp.stack([core, middle])
    weight_rows = weights.reshape(2, genomes // 2)
    weight_column = weights.reshape(genomes, 1)
    field_column = field_a.T

    swap_core = [(c, c ^ 1) for c in range(4)]
    swap_far = [(c, c ^ 2) for c in range(4)]
    inward, across, outward = [(0, 1), (3, 2)], [(1, 2), (2, 1)], [(1, 0), (2, 3)]

    part_1 = first_logits(states_a, couplings)
    in_1 = lax.ppermute(part_1, "row", inward)
    part_2, keep, send = second_logits(where, after(states_a, part_1), states_b, couplings)
    got = lax.ppermute(send, "col", swap_core)
    in_2 = lax.ppermute(part_2, "row", inward)
    both = add(keep, got)
    far = lax.ppermute(both, "col", swap_far)

    near_1 = add(part_1, in_1)
    across_1 = lax.ppermute(near_1, "row", across)
    resid_1 = residual_b(near_1, across_1, field_b, states_b, weight_column, 0)
    out_1 = lax.ppermute(resid_1, "row", outward)
    near_2 = add(part_2, after(in_2, resid_1))
    across_2 = lax.ppermute(near_2, "row", across)
    resid_2 = residual_b(near_2, across_2, field_b, states_b, weight_column, 1)
    out_2 = lax.ppermute(resid_2, "row", outward)

    resid_a = residual_a(where, both, after(far, near_2), field_column, states_a, weight_rows)
    resid_a_other = lax.ppermute(resid_a, "col", swap_core)

    def gradient(resid, out, part):
        return gradient_parts(where, resid_a, resid_a_other, resid, out, states_a, states_b, weight_rows, seq, part)

    got_1 = lax.all_to_all(gradient(resid_1, out_1, 0), "seq", 0, 0)
    got_2 = lax.all_to_all(gradient(resid_2, out_2, 1), "seq", 0, 0)
    return update(lax.axis_index("seq").astype(jnp.int32).reshape(1), (got_1, got_2), couplings)


def solution(mesh):
    placed = (
        P("seq", "row"),
        P("seq", "col"),
        P(None, "row"),
        P(None, "col"),
        P(None, None, "row", "col"),
        P("seq"),
    )
    return jax.shard_map(
        functools.partial(on_device, dict(mesh.shape)),
        mesh=mesh,
        in_specs=placed,
        out_specs=P(None, None, ("row", "seq"), "col"),
        check_vma=False,
    )
```

```python
import functools
import math

import jax
import jax.numpy as jnp
from jax import lax
from jax.experimental import pallas as pl
from jax.experimental.pallas import tpu as pltpu
from jax.sharding import PartitionSpec as P

STATES = 5
FREE = STATES - 1
SHARE = FREE // 2
COMPS = FREE * SHARE + 1
MARGINS = 8

step_scale = 64.0
ridge_weight = 0.002

OFFSET = 51.0 / 256.0
VMEM_LIMIT = 48 * 1024 * 1024

BF16 = jnp.bfloat16
F32 = jnp.float32


def params():
    return pltpu.CompilerParams(vmem_limit_bytes=VMEM_LIMIT)


def vmem():
    return pl.BlockSpec(memory_space=pltpu.VMEM)


def smem():
    return pl.BlockSpec(memory_space=pltpu.SMEM)


def center_hot(states, k):
    return jnp.where(states == k, 1.0 - OFFSET, -OFFSET).astype(BF16)


def whole(*shape):
    return pl.BlockSpec(shape, lambda *_: (0,) * len(shape))


def cost(flops, *arrays):
    return pl.CostEstimate(
        flops=flops, bytes_accessed=sum(x.size * x.dtype.itemsize for x in arrays), transcendentals=0
    )


def logits_a_kernel(where_ref, sb_hbm, j_hbm, keep_ref, send_ref, narrow_ref, own_ref, sb_ref, j_ref, hot_bt, sems):
    genomes, lb = sb_ref.shape
    la = j_ref.shape[2]
    half = genomes // 2
    states_copy = pltpu.make_async_copy(sb_hbm, sb_ref, sems.at[STATES])
    states_copy.start()
    copies = [pltpu.make_async_copy(j_hbm.at[a], j_ref.at[a], sems.at[a]) for a in range(STATES)]
    for copy in copies:
        copy.start()

    states_copy.wait()
    sbt = sb_ref[...].astype(F32).T
    for b in range(STATES):
        hot_bt[pl.ds(b * lb, lb), :] = jnp.where(sbt == float(b), 1.0, 0.0).astype(BF16)

    first = where_ref[0] == 0
    rows = own_ref.shape[2]
    own_rows = pl.ds(pl.multiple_of(where_ref[2] * rows, rows), rows)
    base = None
    for a in range(STATES):
        copies[a].wait()
        blocks = [j_ref[a, b].astype(BF16) for b in range(STATES)]
        for b in range(STATES):
            narrow_ref[b, pl.ds(a * la, la), :] = blocks[b]
            own_ref[a, b] = (1.0 - step_scale * ridge_weight) * j_ref[a, b, own_rows, :]
        part = jnp.dot(jnp.concatenate(blocks, axis=1), hot_bt[...], preferred_element_type=F32)
        if a == 0:
            base = part
        else:
            free = part - base
            low, high = free[:, :half], free[:, half:]
            keep_ref[a - 1] = jnp.where(first, low, high).astype(BF16)
            send_ref[a - 1] = jnp.where(first, high, low).astype(BF16)


def logits_a(where, states_b, couplings, own_rows):
    genomes, lb = states_b.shape
    la = couplings.shape[2]
    out = jax.ShapeDtypeStruct((FREE, la, genomes // 2), BF16)
    return pl.pallas_call(
        logits_a_kernel,
        in_specs=[smem(), pl.BlockSpec(memory_space=pl.ANY), pl.BlockSpec(memory_space=pl.ANY)],
        out_specs=[vmem()] * 4,
        out_shape=[
            out,
            out,
            jax.ShapeDtypeStruct((STATES, STATES * la, lb), BF16),
            jax.ShapeDtypeStruct((STATES, STATES, own_rows, lb), F32),
        ],
        scratch_shapes=[
            pltpu.VMEM((genomes, lb), jnp.int32),
            pltpu.VMEM(couplings.shape, F32),
            pltpu.VMEM((STATES * lb, genomes), BF16),
            pltpu.SemaphoreType.DMA((STATES + 1,)),
        ],
        compiler_params=params(),
        cost_estimate=cost(2 * genomes * la * lb * STATES**2, couplings),
        name="logits_a",
    )(where, states_b, couplings)


def logits_b_kernel(where_ref, sa_ref, narrow_ref, keep_ref, send_ref, hot_a):
    la = sa_ref.shape[1]
    half = keep_ref.shape[1]
    sa = sa_ref[...]
    for a in range(STATES):
        hot_a[:, pl.ds(a * la, la)] = jnp.where(sa == a, 1.0, 0.0).astype(BF16)
    first = lax.rem(where_ref[1], 2) == 0
    base = jnp.dot(hot_a[...], narrow_ref[0], preferred_element_type=F32)
    for b in range(1, STATES):
        free = jnp.dot(hot_a[...], narrow_ref[b], preferred_element_type=F32) - base
        low, high = free[:half], free[half:]
        keep_ref[b - 1] = jnp.where(first, low, high).astype(BF16)
        send_ref[b - 1] = jnp.where(first, high, low).astype(BF16)


def logits_b(where, states_a, narrow):
    genomes, la = states_a.shape
    lb = narrow.shape[2]
    out = jax.ShapeDtypeStruct((FREE, genomes // 2, lb), BF16)
    return pl.pallas_call(
        logits_b_kernel,
        in_specs=[smem(), vmem(), vmem()],
        out_specs=[vmem()] * 2,
        out_shape=[out] * 2,
        scratch_shapes=[pltpu.VMEM((genomes, STATES * la), BF16)],
        compiler_params=params(),
        cost_estimate=cost(2 * genomes * la * lb * STATES**2, narrow),
        name="logits_b",
    )(where, states_a, narrow)


def free_residuals(logits, states, weight):
    top = jnp.maximum(jnp.maximum(logits[0], logits[1]), jnp.maximum(logits[2], logits[3]))
    top = jnp.maximum(top, 0.0)
    expo = [jnp.exp(x - top) for x in logits]
    scale = 1.0 / (expo[0] + expo[1] + expo[2] + expo[3] + jnp.exp(-top))
    return [
        (weight * (expo[k] * scale - jnp.where(states == k + 1, 1.0, 0.0))).astype(BF16) for k in range(FREE)
    ]


def residual_b_kernel(where_ref, mine_ref, other_ref, field_ref, states_ref, weight_ref, keep_ref, send_ref):
    logits = [
        mine_ref[k].astype(F32) + other_ref[k].astype(F32) + (field_ref[k + 1 : k + 2, :] - field_ref[0:1, :])
        for k in range(FREE)
    ]
    resid = free_residuals(logits, states_ref[...], weight_ref[...])
    first = where_ref[3] == 0
    for k in range(SHARE):
        keep_ref[k] = jnp.where(first, resid[k], resid[SHARE + k])
        send_ref[k] = jnp.where(first, resid[SHARE + k], resid[k])


def residual_b(where, mine, other, field_b, states_b, weight_column):
    free, genomes, lb = mine.shape
    out = jax.ShapeDtypeStruct((SHARE, genomes, lb), BF16)
    return pl.pallas_call(
        residual_b_kernel,
        grid_spec=pltpu.PrefetchScalarGridSpec(
            num_scalar_prefetch=1,
            grid=(1,),
            in_specs=[
                whole(free, genomes, lb),
                whole(free, genomes, lb),
                whole(STATES, lb),
                pl.BlockSpec((genomes, lb), lambda i, s: (lax.rem(s[1], 2), 0)),
                pl.BlockSpec((genomes, 1), lambda i, s: (lax.rem(s[1], 2), 0)),
            ],
            out_specs=[whole(*out.shape)] * 2,
        ),
        out_shape=[out] * 2,
        compiler_params=params(),
        cost_estimate=cost(0, mine, other, mine),
        name="residual_b",
    )(where, mine, other, field_b, states_b, weight_column)


def residual_a_kernel(core_ref, mine_ref, other_ref, field_ref, states_ref, weight_ref, out_ref):
    half = mine_ref.shape[2]
    start = pl.multiple_of(core_ref[0] * half, half)
    states = states_ref[pl.ds(start, half), :].astype(F32).T.astype(jnp.int32)
    weight = weight_ref[pl.ds(core_ref[0], 1), :]
    logits = [
        mine_ref[k].astype(F32) + other_ref[k].astype(F32) + (field_ref[:, k + 1 : k + 2] - field_ref[:, 0:1])
        for k in range(FREE)
    ]
    for k, resid in enumerate(free_residuals(logits, states, weight)):
        out_ref[k] = resid


def residual_a(core, mine, other, field_column, states_a, weight_rows):
    return pl.pallas_call(
        residual_a_kernel,
        in_specs=[smem()] + [vmem()] * 5,
        out_specs=vmem(),
        out_shape=jax.ShapeDtypeStruct(mine.shape, BF16),
        compiler_params=params(),
        cost_estimate=cost(0, mine, other, mine),
        name="residual_a",
    )(core, mine, other, field_column, states_a, weight_rows)


def pack_margins(margins, rows):
    high = margins.astype(BF16).astype(F32)
    parts = [high, margins - high]
    if rows > 2 * MARGINS:
        parts.append(jnp.zeros((rows - 2 * MARGINS, margins.shape[1]), F32))
    return jnp.concatenate(parts, axis=0).astype(BF16)


def unpack_margins(tile):
    return tile[:MARGINS] + tile[MARGINS : 2 * MARGINS]


def gradient_kernel(where_ref, ra_ref, ra_other_ref, rb_refs, sa_ref, sb_refs, weight_ref, outs, right, held):
    core, row, place, role = where_ref[0], where_ref[1], where_ref[2], where_ref[3]
    _, side, _, rows, width = held.shape
    genomes, la = sa_ref.shape
    lb = width // 2
    grid = (side, side, rows, width)

    def in_order(second, mine, other):
        return jnp.where(second == 0, mine, other), jnp.where(second == 0, other, mine)

    sat = sa_ref[...].astype(F32).T
    line = lax.broadcasted_iota(jnp.int32, (MARGINS, lb), 0)
    weight_sum = jnp.sum(weight_ref[...], keepdims=True).reshape(1, 1)
    margins = []
    both_sb = in_order(core, sb_refs[0][...], sb_refs[1][...])
    both_rb = zip(in_order(core, rb_refs[0][0][...], rb_refs[1][0][...]), in_order(core, rb_refs[0][1][...], rb_refs[1][1][...]))
    for side_b, (sb, (mine_rb, other_rb)) in enumerate(zip(both_sb, both_rb)):
        margin = jnp.where(line == SHARE, weight_sum, 0.0)
        for b in range(SHARE):
            lanes = pl.ds(b * width + side_b * lb, lb)
            right[pl.ds(0, genomes), lanes] = center_hot(sb, role * SHARE + b + 1)
            for k, resid in enumerate(in_order(lax.rem(row, 2), mine_rb[b], other_rb[b])):
                right[pl.ds(genomes + k * (genomes // 2), genomes // 2), lanes] = resid
                margin = margin + jnp.where(line == b, jnp.sum(resid.astype(F32), axis=0, keepdims=True), 0.0)
        margins.append(margin)
    ones = jnp.ones((MARGINS, genomes), BF16)
    for a in range(FREE):
        resid = jnp.concatenate(in_order(core, ra_ref[a], ra_other_ref[a]), axis=1)
        sums = lax.dot_general(ones, resid, (((1,), (1,)), ((), ())), preferred_element_type=F32)
        margins = [jnp.where(line == SHARE + 1 + a, sums, margin) for margin in margins]
        left = jnp.concatenate([resid, center_hot(sat, float(a + 1))], axis=1)
        grad = jnp.dot(left, right[...], preferred_element_type=F32).astype(BF16)
        for b in range(SHARE):
            held[a * SHARE + b] = grad[:, b * width : (b + 1) * width].reshape(grid)
    held[COMPS - 1] = jnp.broadcast_to(pack_margins(jnp.concatenate(margins, axis=1), rows)[None, None], grid)

    x, y = place // side, lax.rem(place, side)

    @pl.when(role == 0)
    def _():
        for k in range(side):
            for c in range(COMPS):
                outs[k][c] = held[c, lax.rem(x + k, side)]

    @pl.when(role == 1)
    def _():
        for k in range(side):
            for c in range(COMPS):
                outs[k][c] = held[c, :, lax.rem(y + k, side)]


def gradient_parts(where, resid_a, resid_a_other, resid_b, states_a, states_b, weight_rows, side):
    genomes, la = states_a.shape
    lb = states_b[0].shape[1]
    rows = la // (side * side)
    out = jax.ShapeDtypeStruct((COMPS, side, rows, 2 * lb), BF16)
    operands = (resid_a, resid_a_other, *resid_b[0], *resid_b[1], states_a, *states_b, weight_rows)

    def kernel(where_ref, ra, ra_other, rb0, rb1, rb2, rb3, sa, sb0, sb1, weight, *refs):
        outs, scratch = refs[:side], refs[side:]
        gradient_kernel(where_ref, ra, ra_other, ((rb0, rb1), (rb2, rb3)), sa, (sb0, sb1), weight, outs, *scratch)

    return pl.pallas_call(
        kernel,
        in_specs=[smem()] + [vmem()] * len(operands),
        out_specs=[vmem()] * side,
        out_shape=[out] * side,
        scratch_shapes=[
            pltpu.VMEM((2 * genomes, SHARE * 2 * lb), BF16),
            pltpu.VMEM((COMPS, side, side, rows, 2 * lb), BF16),
        ],
        compiler_params=params(),
        cost_estimate=cost(4 * genomes * la * lb * FREE * FREE, *operands),
        name="gradient_parts",
    )(where, *operands)


def add_parts(refs):
    total = [refs[0][c].astype(F32) for c in range(COMPS)]
    for ref in refs[1:]:
        total = [x + ref[c].astype(F32) for c, x in enumerate(total)]
    return total


def middle_kernel(where_ref, *refs):
    side = (len(refs) - 1) // 2
    outs, held = refs[side:-1], refs[-1]
    place, role = where_ref[2], where_ref[3]
    rows = held.shape[2]
    *sums, margins = add_parts(refs[:side])
    for c, value in enumerate(sums):
        held[c] = value.astype(BF16)
    for k in range(side):
        held[COMPS - 1, k] = pack_margins(unpack_margins(margins[k]), rows)
    spot = jnp.where(role == 0, lax.rem(place, side), place // side)
    for k, out in enumerate(outs):
        out[...] = held[:, lax.rem(spot + k, side)]


def middle_sums(where, parts):
    side = len(parts)
    comps, _, rows, width = parts[0].shape
    out = jax.ShapeDtypeStruct((comps, rows, width), BF16)
    return pl.pallas_call(
        middle_kernel,
        in_specs=[smem()] + [vmem()] * side,
        out_specs=[vmem()] * side,
        out_shape=[out] * side,
        scratch_shapes=[pltpu.VMEM((comps, side, rows, width), BF16)],
        compiler_params=params(),
        cost_estimate=cost(0, *parts),
        name="middle_sums",
    )(where, *parts)


def last_kernel(where_ref, *refs):
    *parts, keep_ref, send_ref = refs
    lb = keep_ref.shape[2]
    first = where_ref[0] == 0
    for c, value in enumerate(add_parts(parts)):
        low, high = value[:, :lb], value[:, lb:]
        keep_ref[c] = jnp.where(first, low, high)
        send_ref[c] = jnp.where(first, high, low)


def last_sums(where, parts):
    comps, rows, width = parts[0].shape
    out = jax.ShapeDtypeStruct((comps, rows, width // 2), F32)
    return pl.pallas_call(
        last_kernel,
        in_specs=[smem()] + [vmem()] * len(parts),
        out_specs=[vmem()] * 2,
        out_shape=[out] * 2,
        compiler_params=params(),
        cost_estimate=cost(0, *parts),
        name="last_sums",
    )(where, *parts)


def role_of(core, x, y):
    return (core + x + y) % 2


def send_parts(parts, cols, turn):
    side = len(parts)

    def target(col, place, k):
        x, y = place // side, place % side
        role = role_of(col, x, y)
        x, y = ((x + k) % side, y) if (role + turn) % 2 == 0 else (x, (y + k) % side)
        return (col // 2 * 2 + role_of(role, x, y)) * side * side + x * side + y

    got = list(parts)
    for k in sorted(range(1, side), key=lambda k: -min(k, side - k)):
        pairs = [(col * side * side + p, target(col, p, k)) for col in range(cols) for p in range(side * side)]
        got[k] = lax.ppermute(parts[k], ("col", "seq"), pairs)
    return got


def update_kernel(where_ref, mine_ref, other_ref, own_ref, out_ref):
    first = where_ref[3] == 0
    mine, other = unpack_margins(mine_ref[COMPS - 1]), unpack_margins(other_ref[COMPS - 1])
    _, rows, lb = mine_ref.shape

    def in_order(x, y):
        return jnp.where(first, x, y), jnp.where(first, y, x)

    parts, margins = in_order(mine_ref[...], other_ref[...]), in_order(mine, other)
    total = [parts[b // SHARE][a * SHARE + b % SHARE] for a in range(FREE) for b in range(FREE)]
    row = [margins[b // SHARE][b % SHARE : b % SHARE + 1, :] for b in range(FREE)]
    scale = step_scale / mine[SHARE : SHARE + 1, :]
    line = lax.broadcasted_iota(jnp.int32, (rows, lb), 0)
    lane = lax.broadcasted_iota(jnp.int32, (rows, lb), 1)
    at = lane == line + where_ref[2] * rows
    col = [
        jnp.sum(jnp.where(at, mine[SHARE + 1 + a : SHARE + 2 + a, :], 0.0), axis=1, keepdims=True) for a in range(FREE)
    ]

    def emit(a, b, grad):
        out_ref[a, b] = own_ref[a, b] - scale * grad

    along_b = [None] * FREE
    corner = None
    for a in range(FREE):
        along_a = None
        for b in range(FREE):
            grad = total[a * FREE + b] + OFFSET * (col[a] + row[b])
            emit(a + 1, b + 1, grad)
            along_a = grad if along_a is None else along_a + grad
            along_b[b] = grad if a == 0 else along_b[b] + grad
        edge = col[a] - along_a
        emit(a + 1, 0, edge)
        corner = edge if corner is None else corner + edge
    for b in range(FREE):
        emit(0, b + 1, row[b] - along_b[b])
    emit(0, 0, -(row[0] + row[1] + row[2] + row[3]) - corner)


def update(where, mine, other, own):
    return pl.pallas_call(
        update_kernel,
        in_specs=[smem()] + [vmem()] * 3,
        out_specs=vmem(),
        out_shape=jax.ShapeDtypeStruct(own.shape, F32),
        compiler_params=params(),
        cost_estimate=cost(0, mine, other, own),
        name="update",
    )(where, mine, other, own)


def after(x, *others):
    return lax.optimization_barrier((x,) + others)[0]


def add(x, y):
    return (x.astype(F32) + y.astype(F32)).astype(BF16)


def on_device(sizes, states_a, states_b, field_a, field_b, couplings, weights):
    side = math.isqrt(sizes["seq"])
    genomes = states_a.shape[0]
    index = lambda axis: lax.axis_index(axis).astype(jnp.int32)
    core, place = index("col") % 2, index("seq")
    where = jnp.stack([core, index("row"), place, role_of(core, place // side, place % side)])
    weight_rows = weights.reshape(2, genomes // 2)
    weight_column = weights.reshape(genomes, 1)
    field_column = field_a.T

    def swap(x, axis, distance):
        return lax.ppermute(x, axis, [(k, k ^ distance) for k in range(sizes[axis])])

    keep_a, send_a, narrow, own = logits_a(where, states_b, couplings, states_a.shape[1] // side**2)
    got_a = swap(send_a, "col", 1)
    keep_b, send_b = logits_b(where, states_a, narrow)

    near_a = add(keep_a, after(got_a, keep_b))
    far_a = swap(near_a, "col", 2)
    near_b = add(keep_b, after(swap(send_b, "row", 1), near_a))
    far_b = swap(near_b, "row", 2)

    resid_a = residual_a(where, near_a, far_a, field_column, states_a, weight_rows)
    resid_a_other = swap(resid_a, "col", 1)
    keep_rb, send_rb = residual_b(where, near_b, after(far_b, resid_a), field_b, states_b, weight_column)
    send_rb_other = swap(send_rb, "row", 1)
    keep_rb_other = swap(keep_rb, "row", 1)
    resid_b = (keep_rb, keep_rb_other), (swap(send_rb, "col", 1), swap(send_rb_other, "col", 1))
    both_states_b = states_b, swap(after(states_b, near_b), "col", 1)

    parts = gradient_parts(where, resid_a, resid_a_other, resid_b, states_a, both_states_b, weight_rows, side)
    parts = middle_sums(where, send_parts(parts, sizes["col"], 0))
    mine, send = last_sums(where, send_parts(parts, sizes["col"], 1))
    return update(where, mine, swap(send, "col", 1), own)


def solution(mesh):
    placed = (
        P("seq", "row"),
        P("seq", "col"),
        P(None, "row"),
        P(None, "col"),
        P(None, None, "row", "col"),
        P("seq"),
    )
    return jax.shard_map(
        functools.partial(on_device, dict(mesh.shape)),
        mesh=mesh,
        in_specs=placed,
        out_specs=P(None, None, ("row", "seq"), "col"),
        check_vma=False,
    )
```

```python
import functools
import math

import jax
import jax.numpy as jnp
from jax import lax
from jax.experimental import pallas as pl
from jax.experimental.pallas import tpu as pltpu
from jax.sharding import PartitionSpec as P

STATES = 5
FREE = STATES - 1
SHARE = FREE // 2
COMPS = FREE * SHARE + 1
MARGINS = 8

step_scale = 64.0
ridge_weight = 0.002

OFFSET = 51.0 / 256.0

BF16 = jnp.bfloat16
F32 = jnp.float32


def params(mebibytes=24):
    return pltpu.CompilerParams(vmem_limit_bytes=mebibytes * 1024 * 1024)


def vmem():
    return pl.BlockSpec(memory_space=pltpu.VMEM)


def smem():
    return pl.BlockSpec(memory_space=pltpu.SMEM)


def center_hot(states, k):
    return jnp.where(states == k, 1.0 - OFFSET, -OFFSET).astype(BF16)


def whole(*shape):
    return pl.BlockSpec(shape, lambda *_: (0,) * len(shape))


def cost(flops, *arrays):
    return pl.CostEstimate(
        flops=flops, bytes_accessed=sum(x.size * x.dtype.itemsize for x in arrays), transcendentals=0
    )


def logits_a_kernel(where_ref, sb_hbm, j_hbm, keep_ref, send_ref, narrow_ref, own_ref, sb_ref, j_ref, hot_bt, sems):
    genomes, lb = sb_ref.shape
    la = j_ref.shape[2]
    half = genomes // 2
    states_copy = pltpu.make_async_copy(sb_hbm, sb_ref, sems.at[STATES])
    states_copy.start()
    copies = [pltpu.make_async_copy(j_hbm.at[a], j_ref.at[a], sems.at[a]) for a in range(STATES)]
    for copy in copies:
        copy.start()

    states_copy.wait()
    sbt = sb_ref[...].astype(F32).T
    for b in range(STATES):
        hot_bt[pl.ds(b * lb, lb), :] = jnp.where(sbt == float(b), 1.0, 0.0).astype(BF16)

    first = where_ref[0] == 0
    rows = own_ref.shape[2]
    own_rows = pl.ds(pl.multiple_of(where_ref[2] * rows, rows), rows)
    base = None
    for a in range(STATES):
        copies[a].wait()
        blocks = [j_ref[a, b].astype(BF16) for b in range(STATES)]
        for b in range(STATES):
            narrow_ref[b, pl.ds(a * la, la), :] = blocks[b]
            own_ref[a, b] = (1.0 - step_scale * ridge_weight) * j_ref[a, b, own_rows, :]
        part = jnp.dot(jnp.concatenate(blocks, axis=1), hot_bt[...], preferred_element_type=F32)
        if a == 0:
            base = part
        else:
            free = part - base
            low, high = free[:, :half], free[:, half:]
            keep_ref[a - 1] = jnp.where(first, low, high).astype(BF16)
            send_ref[a - 1] = jnp.where(first, high, low).astype(BF16)


def logits_a(where, states_b, couplings, own_rows):
    genomes, lb = states_b.shape
    la = couplings.shape[2]
    out = jax.ShapeDtypeStruct((FREE, la, genomes // 2), BF16)
    return pl.pallas_call(
        logits_a_kernel,
        in_specs=[smem(), pl.BlockSpec(memory_space=pl.ANY), pl.BlockSpec(memory_space=pl.ANY)],
        out_specs=[vmem()] * 4,
        out_shape=[
            out,
            out,
            jax.ShapeDtypeStruct((STATES, STATES * la, lb), BF16),
            jax.ShapeDtypeStruct((STATES, STATES, own_rows, lb), F32),
        ],
        scratch_shapes=[
            pltpu.VMEM((genomes, lb), jnp.int32),
            pltpu.VMEM(couplings.shape, F32),
            pltpu.VMEM((STATES * lb, genomes), BF16),
            pltpu.SemaphoreType.DMA((STATES + 1,)),
        ],
        compiler_params=params(48),
        cost_estimate=cost(2 * genomes * la * lb * STATES**2, couplings),
        name="logits_a",
    )(where, states_b, couplings)


def logits_b_kernel(where_ref, sa_ref, narrow_ref, keep_ref, send_ref, hot_a):
    la = sa_ref.shape[1]
    half = keep_ref.shape[1]
    sa = sa_ref[...]
    for a in range(STATES):
        hot_a[:, pl.ds(a * la, la)] = jnp.where(sa == a, 1.0, 0.0).astype(BF16)
    first = lax.rem(where_ref[1], 2) == 0
    base = jnp.dot(hot_a[...], narrow_ref[0], preferred_element_type=F32)
    for b in range(1, STATES):
        free = jnp.dot(hot_a[...], narrow_ref[b], preferred_element_type=F32) - base
        low, high = free[:half], free[half:]
        keep_ref[b - 1] = jnp.where(first, low, high).astype(BF16)
        send_ref[b - 1] = jnp.where(first, high, low).astype(BF16)


def logits_b(where, states_a, narrow):
    genomes, la = states_a.shape
    lb = narrow.shape[2]
    out = jax.ShapeDtypeStruct((FREE, genomes // 2, lb), BF16)
    return pl.pallas_call(
        logits_b_kernel,
        in_specs=[smem(), vmem(), vmem()],
        out_specs=[vmem()] * 2,
        out_shape=[out] * 2,
        scratch_shapes=[pltpu.VMEM((genomes, STATES * la), BF16)],
        compiler_params=params(),
        cost_estimate=cost(2 * genomes * la * lb * STATES**2, narrow),
        name="logits_b",
    )(where, states_a, narrow)


def free_residuals(logits, states, weight):
    top = jnp.maximum(jnp.maximum(logits[0], logits[1]), jnp.maximum(logits[2], logits[3]))
    top = jnp.maximum(top, 0.0)
    expo = [jnp.exp(x - top) for x in logits]
    scale = 1.0 / (expo[0] + expo[1] + expo[2] + expo[3] + jnp.exp(-top))
    return [
        (weight * (expo[k] * scale - jnp.where(states == k + 1, 1.0, 0.0))).astype(BF16) for k in range(FREE)
    ]


def residual_b_kernel(where_ref, mine_ref, other_ref, field_ref, states_ref, weight_ref, keep_ref, send_ref):
    logits = [
        mine_ref[k].astype(F32) + other_ref[k].astype(F32) + (field_ref[k + 1 : k + 2, :] - field_ref[0:1, :])
        for k in range(FREE)
    ]
    resid = free_residuals(logits, states_ref[...], weight_ref[...])
    first = where_ref[3] == 0
    for k in range(SHARE):
        keep_ref[k] = jnp.where(first, resid[k], resid[SHARE + k])
        send_ref[k] = jnp.where(first, resid[SHARE + k], resid[k])


def residual_b(where, mine, other, field_b, states_b, weight_column):
    free, genomes, lb = mine.shape
    out = jax.ShapeDtypeStruct((SHARE, genomes, lb), BF16)
    return pl.pallas_call(
        residual_b_kernel,
        grid_spec=pltpu.PrefetchScalarGridSpec(
            num_scalar_prefetch=1,
            grid=(1,),
            in_specs=[
                whole(free, genomes, lb),
                whole(free, genomes, lb),
                whole(STATES, lb),
                whole(genomes, lb),
                pl.BlockSpec((genomes, 1), lambda i, s: (lax.rem(s[1], 2), 0)),
            ],
            out_specs=[whole(*out.shape)] * 2,
        ),
        out_shape=[out] * 2,
        compiler_params=params(),
        cost_estimate=cost(0, mine, other, mine),
        name="residual_b",
    )(where, mine, other, field_b, states_b, weight_column)


def residual_a_kernel(core_ref, mine_ref, other_ref, field_ref, states_ref, weight_ref, out_ref):
    half = mine_ref.shape[2]
    start = pl.multiple_of(core_ref[0] * half, half)
    states = states_ref[pl.ds(start, half), :].astype(F32).T.astype(jnp.int32)
    weight = weight_ref[pl.ds(core_ref[0], 1), :]
    logits = [
        mine_ref[k].astype(F32) + other_ref[k].astype(F32) + (field_ref[:, k + 1 : k + 2] - field_ref[:, 0:1])
        for k in range(FREE)
    ]
    for k, resid in enumerate(free_residuals(logits, states, weight)):
        out_ref[k] = resid


def residual_a(core, mine, other, field_column, states_a, weight_rows):
    return pl.pallas_call(
        residual_a_kernel,
        in_specs=[smem()] + [vmem()] * 5,
        out_specs=vmem(),
        out_shape=jax.ShapeDtypeStruct(mine.shape, BF16),
        compiler_params=params(),
        cost_estimate=cost(0, mine, other, mine),
        name="residual_a",
    )(core, mine, other, field_column, states_a, weight_rows)


def pack_margins(margins, rows):
    high = margins.astype(BF16).astype(F32)
    parts = [high, margins - high]
    if rows > 2 * MARGINS:
        parts.append(jnp.zeros((rows - 2 * MARGINS, margins.shape[1]), F32))
    return jnp.concatenate(parts, axis=0).astype(BF16)


def unpack_margins(tile):
    return tile[:MARGINS] + tile[MARGINS : 2 * MARGINS]


def in_order(second, mine, other):
    return jnp.where(second == 0, mine, other), jnp.where(second == 0, other, mine)


def operands_kernel(where_ref, sa_ref, sb_ref, sb_far_ref, left_ref, right_ref, half_ref):
    core, role = where_ref[0], where_ref[3]
    lb = sb_ref.shape[1]
    half = half_ref.shape[0]
    half_ref[...] = sb_ref[pl.ds(pl.multiple_of(lax.rem(where_ref[1], 2) * half, half), half), :]
    sat = sa_ref[...].astype(F32).T
    for a in range(FREE):
        left_ref[a] = center_hot(sat, float(a + 1))
    for side_b, sb in enumerate(in_order(core, sb_ref[...], sb_far_ref[...])):
        for b in range(SHARE):
            right_ref[:, pl.ds((2 * b + side_b) * lb, lb)] = center_hot(sb, role * SHARE + b + 1)


def gradient_operands(where, states_a, states_b, states_b_far):
    genomes, la = states_a.shape
    shapes = [
        jax.ShapeDtypeStruct((FREE, la, genomes), BF16),
        jax.ShapeDtypeStruct((genomes, SHARE * 2 * states_b.shape[1]), BF16),
        jax.ShapeDtypeStruct((genomes // 2, states_b.shape[1]), jnp.int32),
    ]
    return pl.pallas_call(
        operands_kernel,
        in_specs=[smem()] + [vmem()] * 3,
        out_specs=[vmem()] * 3,
        out_shape=shapes,
        compiler_params=params(),
        cost_estimate=cost(0, *shapes),
        name="gradient_operands",
    )(where, states_a, states_b, states_b_far)


def gradient_kernel(where_ref, ra_ref, ra_other_ref, rb_refs, left_ref, right_ref, weight_ref, outs, right, held):
    core, row, place, role = where_ref[0], where_ref[1], where_ref[2], where_ref[3]
    _, side, _, rows, width = held.shape
    genomes = right.shape[0]
    lb = width // 2
    grid = (side, side, rows, width)

    line = lax.broadcasted_iota(jnp.int32, (MARGINS, lb), 0)
    weight_sum = jnp.sum(weight_ref[...], keepdims=True).reshape(1, 1)
    margins = []
    both_rb = zip(in_order(core, rb_refs[0][0][...], rb_refs[1][0][...]), in_order(core, rb_refs[0][1][...], rb_refs[1][1][...]))
    for side_b, (mine_rb, other_rb) in enumerate(both_rb):
        margin = jnp.where(line == SHARE, weight_sum, 0.0)
        for b in range(SHARE):
            lanes = pl.ds(b * width + side_b * lb, lb)
            for k, resid in enumerate(in_order(lax.rem(row, 2), mine_rb[b], other_rb[b])):
                right[pl.ds(k * (genomes // 2), genomes // 2), lanes] = resid
                margin = margin + jnp.where(line == b, jnp.sum(resid.astype(F32), axis=0, keepdims=True), 0.0)
        margins.append(margin)
    ones = jnp.ones((MARGINS, genomes), BF16)
    for a in range(FREE):
        resid = jnp.concatenate(in_order(core, ra_ref[a], ra_other_ref[a]), axis=1)
        sums = lax.dot_general(ones, resid, (((1,), (1,)), ((), ())), preferred_element_type=F32)
        margins = [jnp.where(line == SHARE + 1 + a, sums, margin) for margin in margins]
        grad = jnp.dot(resid, right_ref[...], preferred_element_type=F32)
        grad = (grad + jnp.dot(left_ref[a], right[...], preferred_element_type=F32)).astype(BF16)
        for b in range(SHARE):
            held[a * SHARE + b] = grad[:, b * width : (b + 1) * width].reshape(grid)
    held[COMPS - 1] = jnp.broadcast_to(pack_margins(jnp.concatenate(margins, axis=1), rows)[None, None], grid)

    x, y = place // side, lax.rem(place, side)

    @pl.when(role == 0)
    def _():
        for k in range(side):
            for c in range(COMPS):
                outs[k][c] = held[c, lax.rem(x + k, side)]

    @pl.when(role == 1)
    def _():
        for k in range(side):
            for c in range(COMPS):
                outs[k][c] = held[c, :, lax.rem(y + k, side)]


def gradient_parts(where, resid_a, resid_a_other, resid_b, hot, weight_rows, side):
    _, la, genomes = hot[0].shape
    lb = hot[1].shape[1] // (2 * SHARE)
    rows = la // (side * side)
    out = jax.ShapeDtypeStruct((COMPS, side, rows, 2 * lb), BF16)
    operands = (resid_a, resid_a_other, *resid_b[0], *resid_b[1], *hot, weight_rows)

    def kernel(where_ref, ra, ra_other, rb0, rb1, rb2, rb3, left, hot_b, weight, *refs):
        outs, scratch = refs[:side], refs[side:]
        gradient_kernel(where_ref, ra, ra_other, ((rb0, rb1), (rb2, rb3)), left, hot_b, weight, outs, *scratch)

    return pl.pallas_call(
        kernel,
        in_specs=[smem()] + [vmem()] * len(operands),
        out_specs=[vmem()] * side,
        out_shape=[out] * side,
        scratch_shapes=[
            pltpu.VMEM((genomes, SHARE * 2 * lb), BF16),
            pltpu.VMEM((COMPS, side, side, rows, 2 * lb), BF16),
        ],
        compiler_params=params(),
        cost_estimate=cost(4 * genomes * la * lb * FREE * FREE, *operands),
        name="gradient_parts",
    )(where, *operands)


def add_parts(refs):
    total = [refs[0][c].astype(F32) for c in range(COMPS)]
    for ref in refs[1:]:
        total = [x + ref[c].astype(F32) for c, x in enumerate(total)]
    return total


def middle_kernel(where_ref, *refs):
    side = (len(refs) - 1) // 2
    outs, held = refs[side:-1], refs[-1]
    place, role = where_ref[2], where_ref[3]
    rows = held.shape[2]
    *sums, margins = add_parts(refs[:side])
    for c, value in enumerate(sums):
        held[c] = value.astype(BF16)
    for k in range(side):
        held[COMPS - 1, k] = pack_margins(unpack_margins(margins[k]), rows)
    spot = jnp.where(role == 0, lax.rem(place, side), place // side)
    for k, out in enumerate(outs):
        out[...] = held[:, lax.rem(spot + k, side)]


def middle_sums(where, parts):
    side = len(parts)
    comps, _, rows, width = parts[0].shape
    out = jax.ShapeDtypeStruct((comps, rows, width), BF16)
    return pl.pallas_call(
        middle_kernel,
        in_specs=[smem()] + [vmem()] * side,
        out_specs=[vmem()] * side,
        out_shape=[out] * side,
        scratch_shapes=[pltpu.VMEM((comps, side, rows, width), BF16)],
        compiler_params=params(),
        cost_estimate=cost(0, *parts),
        name="middle_sums",
    )(where, *parts)


def last_kernel(where_ref, *refs):
    *parts, keep_ref, send_ref = refs
    lb = keep_ref.shape[2]
    first = where_ref[0] == 0
    for c, value in enumerate(add_parts(parts)):
        low, high = value[:, :lb], value[:, lb:]
        keep_ref[c] = jnp.where(first, low, high)
        send_ref[c] = jnp.where(first, high, low)


def last_sums(where, parts):
    comps, rows, width = parts[0].shape
    out = jax.ShapeDtypeStruct((comps, rows, width // 2), F32)
    return pl.pallas_call(
        last_kernel,
        in_specs=[smem()] + [vmem()] * len(parts),
        out_specs=[vmem()] * 2,
        out_shape=[out] * 2,
        compiler_params=params(),
        cost_estimate=cost(0, *parts),
        name="last_sums",
    )(where, *parts)


def role_of(core, x, y):
    return (core + x + y) % 2


def send_parts(parts, cols, turn):
    side = len(parts)

    def target(col, place, k):
        x, y = place // side, place % side
        role = role_of(col, x, y)
        x, y = ((x + k) % side, y) if (role + turn) % 2 == 0 else (x, (y + k) % side)
        return (col // 2 * 2 + role_of(role, x, y)) * side * side + x * side + y

    got = list(parts)
    for k in sorted(range(1, side), key=lambda k: -min(k, side - k)):
        pairs = [(col * side * side + p, target(col, p, k)) for col in range(cols) for p in range(side * side)]
        got[k] = lax.ppermute(parts[k], ("col", "seq"), pairs)
    return got


def update_kernel(where_ref, mine_ref, other_ref, own_ref, out_ref):
    first = where_ref[3] == 0
    mine, other = unpack_margins(mine_ref[COMPS - 1]), unpack_margins(other_ref[COMPS - 1])
    _, rows, lb = mine_ref.shape

    def in_order(x, y):
        return jnp.where(first, x, y), jnp.where(first, y, x)

    parts, margins = in_order(mine_ref[...], other_ref[...]), in_order(mine, other)
    total = [parts[b // SHARE][a * SHARE + b % SHARE] for a in range(FREE) for b in range(FREE)]
    row = [margins[b // SHARE][b % SHARE : b % SHARE + 1, :] for b in range(FREE)]
    scale = step_scale / mine[SHARE : SHARE + 1, :]
    line = lax.broadcasted_iota(jnp.int32, (rows, lb), 0)
    lane = lax.broadcasted_iota(jnp.int32, (rows, lb), 1)
    at = lane == line + where_ref[2] * rows
    col = [
        jnp.sum(jnp.where(at, mine[SHARE + 1 + a : SHARE + 2 + a, :], 0.0), axis=1, keepdims=True) for a in range(FREE)
    ]

    def emit(a, b, grad):
        out_ref[a, b] = own_ref[a, b] - scale * grad

    along_b = [None] * FREE
    corner = None
    for a in range(FREE):
        along_a = None
        for b in range(FREE):
            grad = total[a * FREE + b] + OFFSET * (col[a] + row[b])
            emit(a + 1, b + 1, grad)
            along_a = grad if along_a is None else along_a + grad
            along_b[b] = grad if a == 0 else along_b[b] + grad
        edge = col[a] - along_a
        emit(a + 1, 0, edge)
        corner = edge if corner is None else corner + edge
    for b in range(FREE):
        emit(0, b + 1, row[b] - along_b[b])
    emit(0, 0, -(row[0] + row[1] + row[2] + row[3]) - corner)


def update(where, mine, other, own):
    return pl.pallas_call(
        update_kernel,
        in_specs=[smem()] + [vmem()] * 3,
        out_specs=vmem(),
        out_shape=jax.ShapeDtypeStruct(own.shape, F32),
        compiler_params=params(),
        cost_estimate=cost(0, mine, other, own),
        name="update",
    )(where, mine, other, own)


def after(x, *others):
    return lax.optimization_barrier((x,) + others)[0]


def add(x, y):
    return (x.astype(F32) + y.astype(F32)).astype(BF16)


def on_device(sizes, states_a, states_b, field_a, field_b, couplings, weights):
    side = math.isqrt(sizes["seq"])
    genomes = states_a.shape[0]
    index = lambda axis: lax.axis_index(axis).astype(jnp.int32)
    core, place = index("col") % 2, index("seq")
    where = jnp.stack([core, index("row"), place, role_of(core, place // side, place % side)])
    weight_rows = weights.reshape(2, genomes // 2)
    weight_column = weights.reshape(genomes, 1)
    field_column = field_a.T

    def swap(x, axis, distance):
        return lax.ppermute(x, axis, [(k, k ^ distance) for k in range(sizes[axis])])

    keep_a, send_a, narrow, own = logits_a(where, states_b, couplings, states_a.shape[1] // side**2)
    got_a = swap(send_a, "col", 1)
    keep_b, send_b = logits_b(where, states_a, narrow)

    near_a = add(keep_a, after(got_a, keep_b))
    far_a = swap(near_a, "col", 2)
    near_b = add(keep_b, after(swap(send_b, "row", 1), near_a))
    far_b = swap(near_b, "row", 2)

    resid_a = residual_a(where, near_a, far_a, field_column, states_a, weight_rows)
    resid_a_other = swap(resid_a, "col", 1)
    *hot, half_b = gradient_operands(where, states_a, states_b, swap(after(states_b, near_b), "col", 1))
    keep_rb, send_rb = residual_b(where, near_b, after(far_b, resid_a, hot[0]), field_b, half_b, weight_column)
    send_rb_other = swap(send_rb, "row", 1)
    keep_rb_other = swap(keep_rb, "row", 1)
    resid_b = (keep_rb, keep_rb_other), (swap(send_rb, "col", 1), swap(send_rb_other, "col", 1))

    parts = gradient_parts(where, resid_a, resid_a_other, resid_b, hot, weight_rows, side)
    parts = middle_sums(where, send_parts(parts, sizes["col"], 0))
    mine, send = last_sums(where, send_parts(parts, sizes["col"], 1))
    return update(where, mine, swap(send, "col", 1), own)


def solution(mesh):
    placed = (
        P("seq", "row"),
        P("seq", "col"),
        P(None, "row"),
        P(None, "col"),
        P(None, None, "row", "col"),
        P("seq"),
    )
    return jax.shard_map(
        functools.partial(on_device, dict(mesh.shape)),
        mesh=mesh,
        in_specs=placed,
        out_specs=P(None, None, ("row", "seq"), "col"),
        check_vma=False,
    )
```

```python
import functools
import math

import jax
import jax.numpy as jnp
from jax import lax
from jax.experimental import pallas as pl
from jax.experimental.pallas import tpu as pltpu
from jax.sharding import PartitionSpec as P

STATES = 5
FREE = STATES - 1
SHARE = FREE // 2
COMPS = FREE * SHARE + 1
MARGINS = 8

step_scale = 64.0
ridge_weight = 0.002

OFFSET = 51.0 / 256.0

BF16 = jnp.bfloat16
F32 = jnp.float32


def params(mebibytes=24):
    return pltpu.CompilerParams(vmem_limit_bytes=mebibytes * 1024 * 1024)


def vmem():
    return pl.BlockSpec(memory_space=pltpu.VMEM)


def smem():
    return pl.BlockSpec(memory_space=pltpu.SMEM)


def center_hot(states, k):
    return jnp.where(states == k, 1.0 - OFFSET, -OFFSET).astype(BF16)


def whole(*shape):
    return pl.BlockSpec(shape, lambda *_: (0,) * len(shape))


def cost(flops, *arrays):
    return pl.CostEstimate(
        flops=flops, bytes_accessed=sum(x.size * x.dtype.itemsize for x in arrays), transcendentals=0
    )


def logits_a_kernel(where_ref, sb_hbm, j_hbm, keep_ref, send_ref, narrow_ref, sb_ref, j_ref, hot_bt, sems):
    genomes, lb = sb_ref.shape
    la = j_ref.shape[2]
    half = genomes // 2
    states_copy = pltpu.make_async_copy(sb_hbm, sb_ref, sems.at[STATES])
    states_copy.start()
    copies = [pltpu.make_async_copy(j_hbm.at[a], j_ref.at[a], sems.at[a]) for a in range(STATES)]
    for copy in copies:
        copy.start()

    states_copy.wait()
    sbt = sb_ref[...].astype(F32).T
    for b in range(STATES):
        hot_bt[pl.ds(b * lb, lb), :] = jnp.where(sbt == float(b), 1.0, 0.0).astype(BF16)

    first = where_ref[0] == 0
    base = None
    for a in range(STATES):
        copies[a].wait()
        blocks = [j_ref[a, b].astype(BF16) for b in range(STATES)]
        for b in range(STATES):
            narrow_ref[b, pl.ds(a * la, la), :] = blocks[b]
        part = jnp.dot(jnp.concatenate(blocks, axis=1), hot_bt[...], preferred_element_type=F32)
        if a == 0:
            base = part
        else:
            free = part - base
            low, high = free[:, :half], free[:, half:]
            keep_ref[a - 1] = jnp.where(first, low, high).astype(BF16)
            send_ref[a - 1] = jnp.where(first, high, low).astype(BF16)


def logits_a(where, states_b, couplings):
    genomes, lb = states_b.shape
    la = couplings.shape[2]
    out = jax.ShapeDtypeStruct((FREE, la, genomes // 2), BF16)
    return pl.pallas_call(
        logits_a_kernel,
        in_specs=[smem(), pl.BlockSpec(memory_space=pl.ANY), pl.BlockSpec(memory_space=pl.ANY)],
        out_specs=[vmem()] * 3,
        out_shape=[out, out, jax.ShapeDtypeStruct((STATES, STATES * la, lb), BF16)],
        scratch_shapes=[
            pltpu.VMEM((genomes, lb), jnp.int32),
            pltpu.VMEM(couplings.shape, F32),
            pltpu.VMEM((STATES * lb, genomes), BF16),
            pltpu.SemaphoreType.DMA((STATES + 1,)),
        ],
        compiler_params=params(48),
        cost_estimate=cost(2 * genomes * la * lb * STATES**2, couplings),
        name="logits_a",
    )(where, states_b, couplings)


def logits_b_kernel(where_ref, sa_ref, narrow_ref, keep_ref, send_ref, hot_a):
    la = sa_ref.shape[1]
    half = keep_ref.shape[1]
    sa = sa_ref[...]
    for a in range(STATES):
        hot_a[:, pl.ds(a * la, la)] = jnp.where(sa == a, 1.0, 0.0).astype(BF16)
    first = lax.rem(where_ref[1], 2) == 0
    base = jnp.dot(hot_a[...], narrow_ref[0], preferred_element_type=F32)
    for b in range(1, STATES):
        free = jnp.dot(hot_a[...], narrow_ref[b], preferred_element_type=F32) - base
        low, high = free[:half], free[half:]
        keep_ref[b - 1] = jnp.where(first, low, high).astype(BF16)
        send_ref[b - 1] = jnp.where(first, high, low).astype(BF16)


def logits_b(where, states_a, narrow):
    genomes, la = states_a.shape
    lb = narrow.shape[2]
    out = jax.ShapeDtypeStruct((FREE, genomes // 2, lb), BF16)
    return pl.pallas_call(
        logits_b_kernel,
        in_specs=[smem(), vmem(), vmem()],
        out_specs=[vmem()] * 2,
        out_shape=[out] * 2,
        scratch_shapes=[pltpu.VMEM((genomes, STATES * la), BF16)],
        compiler_params=params(),
        cost_estimate=cost(2 * genomes * la * lb * STATES**2, narrow),
        name="logits_b",
    )(where, states_a, narrow)


def free_residuals(logits, states, weight):
    top = jnp.maximum(jnp.maximum(logits[0], logits[1]), jnp.maximum(logits[2], logits[3]))
    top = jnp.maximum(top, 0.0)
    expo = [jnp.exp(x - top) for x in logits]
    scale = 1.0 / (expo[0] + expo[1] + expo[2] + expo[3] + jnp.exp(-top))
    return [
        (weight * (expo[k] * scale - jnp.where(states == k + 1, 1.0, 0.0))).astype(BF16) for k in range(FREE)
    ]


def residual_b_kernel(where_ref, mine_ref, other_ref, field_ref, states_ref, weight_ref, keep_ref, send_ref):
    logits = [
        mine_ref[k].astype(F32) + other_ref[k].astype(F32) + (field_ref[k + 1 : k + 2, :] - field_ref[0:1, :])
        for k in range(FREE)
    ]
    resid = free_residuals(logits, states_ref[...], weight_ref[...])
    first = where_ref[3] == 0
    for k in range(SHARE):
        keep_ref[k] = jnp.where(first, resid[k], resid[SHARE + k])
        send_ref[k] = jnp.where(first, resid[SHARE + k], resid[k])


def residual_b(where, mine, other, field_b, states_b, weight_column):
    free, genomes, lb = mine.shape
    out = jax.ShapeDtypeStruct((SHARE, genomes, lb), BF16)
    return pl.pallas_call(
        residual_b_kernel,
        grid_spec=pltpu.PrefetchScalarGridSpec(
            num_scalar_prefetch=1,
            grid=(1,),
            in_specs=[
                whole(free, genomes, lb),
                whole(free, genomes, lb),
                whole(STATES, lb),
                whole(genomes, lb),
                pl.BlockSpec((genomes, 1), lambda i, s: (lax.rem(s[1], 2), 0)),
            ],
            out_specs=[whole(*out.shape)] * 2,
        ),
        out_shape=[out] * 2,
        compiler_params=params(),
        cost_estimate=cost(0, mine, other, mine),
        name="residual_b",
    )(where, mine, other, field_b, states_b, weight_column)


def residual_a_kernel(core_ref, mine_ref, other_ref, field_ref, states_ref, weight_ref, out_ref):
    half = mine_ref.shape[2]
    start = pl.multiple_of(core_ref[0] * half, half)
    states = states_ref[pl.ds(start, half), :].astype(F32).T.astype(jnp.int32)
    weight = weight_ref[pl.ds(core_ref[0], 1), :]
    logits = [
        mine_ref[k].astype(F32) + other_ref[k].astype(F32) + (field_ref[:, k + 1 : k + 2] - field_ref[:, 0:1])
        for k in range(FREE)
    ]
    for k, resid in enumerate(free_residuals(logits, states, weight)):
        out_ref[k] = resid


def residual_a(core, mine, other, field_column, states_a, weight_rows):
    return pl.pallas_call(
        residual_a_kernel,
        in_specs=[smem()] + [vmem()] * 5,
        out_specs=vmem(),
        out_shape=jax.ShapeDtypeStruct(mine.shape, BF16),
        compiler_params=params(),
        cost_estimate=cost(0, mine, other, mine),
        name="residual_a",
    )(core, mine, other, field_column, states_a, weight_rows)


def pack_margins(margins, rows):
    high = margins.astype(BF16).astype(F32)
    parts = [high, margins - high]
    if rows > 2 * MARGINS:
        parts.append(jnp.zeros((rows - 2 * MARGINS, margins.shape[1]), F32))
    return jnp.concatenate(parts, axis=0).astype(BF16)


def unpack_margins(tile):
    return tile[:MARGINS] + tile[MARGINS : 2 * MARGINS]


def in_order(second, mine, other):
    return jnp.where(second == 0, mine, other), jnp.where(second == 0, other, mine)


def operands_kernel(where_ref, sa_ref, sb_ref, sb_far_ref, j_hbm, left_ref, right_ref, half_ref, own_ref, block, sem):
    rows = own_ref.shape[2]
    start = pl.multiple_of(where_ref[2] * rows, rows)
    copy = pltpu.make_async_copy(j_hbm.at[:, :, pl.ds(start, rows), :], block, sem)
    copy.start()
    core, role = where_ref[0], where_ref[3]
    lb = sb_ref.shape[1]
    half = half_ref.shape[0]
    half_ref[...] = sb_ref[pl.ds(pl.multiple_of(lax.rem(where_ref[1], 2) * half, half), half), :]
    sat = sa_ref[...].astype(F32).T
    for a in range(FREE):
        left_ref[a] = center_hot(sat, float(a + 1))
    for side_b, sb in enumerate(in_order(core, sb_ref[...], sb_far_ref[...])):
        for b in range(SHARE):
            right_ref[:, pl.ds((2 * b + side_b) * lb, lb)] = center_hot(sb, role * SHARE + b + 1)
    copy.wait()
    own_ref[...] = (1.0 - step_scale * ridge_weight) * block[...]


def gradient_operands(where, states_a, states_b, states_b_far, couplings, rows):
    genomes, la = states_a.shape
    shapes = [
        jax.ShapeDtypeStruct((FREE, la, genomes), BF16),
        jax.ShapeDtypeStruct((genomes, SHARE * 2 * states_b.shape[1]), BF16),
        jax.ShapeDtypeStruct((genomes // 2, states_b.shape[1]), jnp.int32),
        jax.ShapeDtypeStruct((STATES, STATES, rows, states_b.shape[1]), F32),
    ]
    return pl.pallas_call(
        operands_kernel,
        in_specs=[smem()] + [vmem()] * 3 + [pl.BlockSpec(memory_space=pl.ANY)],
        out_specs=[vmem()] * 4,
        out_shape=shapes,
        scratch_shapes=[pltpu.VMEM(shapes[3].shape, F32), pltpu.SemaphoreType.DMA(())],
        compiler_params=params(),
        cost_estimate=cost(0, *shapes),
        name="gradient_operands",
    )(where, states_a, states_b, states_b_far, couplings)


def gradient_kernel(where_ref, ra_ref, ra_other_ref, rb_refs, left_ref, right_ref, weight_ref, outs, right, held):
    core, row, place, role = where_ref[0], where_ref[1], where_ref[2], where_ref[3]
    _, side, _, rows, width = held.shape
    genomes = right.shape[0]
    lb = width // 2
    grid = (side, side, rows, width)

    line = lax.broadcasted_iota(jnp.int32, (MARGINS, lb), 0)
    weight_sum = jnp.sum(weight_ref[...], keepdims=True).reshape(1, 1)
    margins = []
    both_rb = zip(in_order(core, rb_refs[0][0][...], rb_refs[1][0][...]), in_order(core, rb_refs[0][1][...], rb_refs[1][1][...]))
    for side_b, (mine_rb, other_rb) in enumerate(both_rb):
        margin = jnp.where(line == SHARE, weight_sum, 0.0)
        for b in range(SHARE):
            lanes = pl.ds(b * width + side_b * lb, lb)
            for k, resid in enumerate(in_order(lax.rem(row, 2), mine_rb[b], other_rb[b])):
                right[pl.ds(k * (genomes // 2), genomes // 2), lanes] = resid
                margin = margin + jnp.where(line == b, jnp.sum(resid.astype(F32), axis=0, keepdims=True), 0.0)
        margins.append(margin)
    ones = jnp.ones((MARGINS, genomes), BF16)
    for a in range(FREE):
        resid = jnp.concatenate(in_order(core, ra_ref[a], ra_other_ref[a]), axis=1)
        sums = lax.dot_general(ones, resid, (((1,), (1,)), ((), ())), preferred_element_type=F32)
        margins = [jnp.where(line == SHARE + 1 + a, sums, margin) for margin in margins]
        grad = jnp.dot(resid, right_ref[...], preferred_element_type=F32)
        grad = (grad + jnp.dot(left_ref[a], right[...], preferred_element_type=F32)).astype(BF16)
        for b in range(SHARE):
            held[a * SHARE + b] = grad[:, b * width : (b + 1) * width].reshape(grid)
    held[COMPS - 1] = jnp.broadcast_to(pack_margins(jnp.concatenate(margins, axis=1), rows)[None, None], grid)

    x, y = place // side, lax.rem(place, side)

    @pl.when(role == 0)
    def _():
        for k in range(side):
            for c in range(COMPS):
                outs[k][c] = held[c, lax.rem(x + k, side)]

    @pl.when(role == 1)
    def _():
        for k in range(side):
            for c in range(COMPS):
                outs[k][c] = held[c, :, lax.rem(y + k, side)]


def gradient_parts(where, resid_a, resid_a_other, resid_b, hot, weight_rows, side):
    _, la, genomes = hot[0].shape
    lb = hot[1].shape[1] // (2 * SHARE)
    rows = la // (side * side)
    out = jax.ShapeDtypeStruct((COMPS, side, rows, 2 * lb), BF16)
    operands = (resid_a, resid_a_other, *resid_b[0], *resid_b[1], *hot, weight_rows)

    def kernel(where_ref, ra, ra_other, rb0, rb1, rb2, rb3, left, hot_b, weight, *refs):
        outs, scratch = refs[:side], refs[side:]
        gradient_kernel(where_ref, ra, ra_other, ((rb0, rb1), (rb2, rb3)), left, hot_b, weight, outs, *scratch)

    return pl.pallas_call(
        kernel,
        in_specs=[smem()] + [vmem()] * len(operands),
        out_specs=[vmem()] * side,
        out_shape=[out] * side,
        scratch_shapes=[
            pltpu.VMEM((genomes, SHARE * 2 * lb), BF16),
            pltpu.VMEM((COMPS, side, side, rows, 2 * lb), BF16),
        ],
        compiler_params=params(),
        cost_estimate=cost(4 * genomes * la * lb * FREE * FREE, *operands),
        name="gradient_parts",
    )(where, *operands)


def add_parts(refs):
    total = [refs[0][c].astype(F32) for c in range(COMPS)]
    for ref in refs[1:]:
        total = [x + ref[c].astype(F32) for c, x in enumerate(total)]
    return total


def middle_kernel(where_ref, *refs):
    side = (len(refs) - 1) // 2
    outs, held = refs[side:-1], refs[-1]
    place, role = where_ref[2], where_ref[3]
    rows = held.shape[2]
    *sums, margins = add_parts(refs[:side])
    for c, value in enumerate(sums):
        held[c] = value.astype(BF16)
    for k in range(side):
        held[COMPS - 1, k] = pack_margins(unpack_margins(margins[k]), rows)
    spot = jnp.where(role == 0, lax.rem(place, side), place // side)
    for k, out in enumerate(outs):
        out[...] = held[:, lax.rem(spot + k, side)]


def middle_sums(where, parts):
    side = len(parts)
    comps, _, rows, width = parts[0].shape
    out = jax.ShapeDtypeStruct((comps, rows, width), BF16)
    return pl.pallas_call(
        middle_kernel,
        in_specs=[smem()] + [vmem()] * side,
        out_specs=[vmem()] * side,
        out_shape=[out] * side,
        scratch_shapes=[pltpu.VMEM((comps, side, rows, width), BF16)],
        compiler_params=params(),
        cost_estimate=cost(0, *parts),
        name="middle_sums",
    )(where, *parts)


def last_kernel(where_ref, *refs):
    *parts, keep_ref, send_ref = refs
    lb = keep_ref.shape[2]
    first = where_ref[0] == 0
    for c, value in enumerate(add_parts(parts)):
        low, high = value[:, :lb], value[:, lb:]
        keep_ref[c] = jnp.where(first, low, high)
        send_ref[c] = jnp.where(first, high, low)


def last_sums(where, parts):
    comps, rows, width = parts[0].shape
    out = jax.ShapeDtypeStruct((comps, rows, width // 2), F32)
    return pl.pallas_call(
        last_kernel,
        in_specs=[smem()] + [vmem()] * len(parts),
        out_specs=[vmem()] * 2,
        out_shape=[out] * 2,
        compiler_params=params(),
        cost_estimate=cost(0, *parts),
        name="last_sums",
    )(where, *parts)


def role_of(core, x, y):
    return (core + x + y) % 2


def send_parts(parts, cols, turn):
    side = len(parts)

    def target(col, place, k):
        x, y = place // side, place % side
        role = role_of(col, x, y)
        x, y = ((x + k) % side, y) if (role + turn) % 2 == 0 else (x, (y + k) % side)
        return (col // 2 * 2 + role_of(role, x, y)) * side * side + x * side + y

    got = list(parts)
    for k in sorted(range(1, side), key=lambda k: -min(k, side - k)):
        pairs = [(col * side * side + p, target(col, p, k)) for col in range(cols) for p in range(side * side)]
        got[k] = lax.ppermute(parts[k], ("col", "seq"), pairs)
    return got


def update_kernel(where_ref, mine_ref, other_ref, own_ref, out_ref):
    first = where_ref[3] == 0
    mine, other = unpack_margins(mine_ref[COMPS - 1]), unpack_margins(other_ref[COMPS - 1])
    _, rows, lb = mine_ref.shape

    def in_order(x, y):
        return jnp.where(first, x, y), jnp.where(first, y, x)

    parts, margins = in_order(mine_ref[...], other_ref[...]), in_order(mine, other)
    total = [parts[b // SHARE][a * SHARE + b % SHARE] for a in range(FREE) for b in range(FREE)]
    row = [margins[b // SHARE][b % SHARE : b % SHARE + 1, :] for b in range(FREE)]
    scale = step_scale / mine[SHARE : SHARE + 1, :]
    line = lax.broadcasted_iota(jnp.int32, (rows, lb), 0)
    lane = lax.broadcasted_iota(jnp.int32, (rows, lb), 1)
    at = lane == line + where_ref[2] * rows
    col = [
        jnp.sum(jnp.where(at, mine[SHARE + 1 + a : SHARE + 2 + a, :], 0.0), axis=1, keepdims=True) for a in range(FREE)
    ]

    def emit(a, b, grad):
        out_ref[a, b] = own_ref[a, b] - scale * grad

    along_b = [None] * FREE
    corner = None
    for a in range(FREE):
        along_a = None
        for b in range(FREE):
            grad = total[a * FREE + b] + OFFSET * (col[a] + row[b])
            emit(a + 1, b + 1, grad)
            along_a = grad if along_a is None else along_a + grad
            along_b[b] = grad if a == 0 else along_b[b] + grad
        edge = col[a] - along_a
        emit(a + 1, 0, edge)
        corner = edge if corner is None else corner + edge
    for b in range(FREE):
        emit(0, b + 1, row[b] - along_b[b])
    emit(0, 0, -(row[0] + row[1] + row[2] + row[3]) - corner)


def update(where, mine, other, own):
    return pl.pallas_call(
        update_kernel,
        in_specs=[smem()] + [vmem()] * 3,
        out_specs=vmem(),
        out_shape=jax.ShapeDtypeStruct(own.shape, F32),
        compiler_params=params(),
        cost_estimate=cost(0, mine, other, own),
        name="update",
    )(where, mine, other, own)


def after(x, *others):
    return lax.optimization_barrier((x,) + others)[0]


def add(x, y):
    return (x.astype(F32) + y.astype(F32)).astype(BF16)


def on_device(sizes, states_a, states_b, field_a, field_b, couplings, weights):
    side = math.isqrt(sizes["seq"])
    genomes = states_a.shape[0]
    index = lambda axis: lax.axis_index(axis).astype(jnp.int32)
    core, place = index("col") % 2, index("seq")
    where = jnp.stack([core, index("row"), place, role_of(core, place // side, place % side)])
    weight_rows = weights.reshape(2, genomes // 2)
    weight_column = weights.reshape(genomes, 1)
    field_column = field_a.T

    def swap(x, axis, distance):
        return lax.ppermute(x, axis, [(k, k ^ distance) for k in range(sizes[axis])])

    keep_a, send_a, narrow = logits_a(where, states_b, couplings)
    got_a = swap(send_a, "col", 1)
    keep_b, send_b = logits_b(where, states_a, narrow)

    near_a = add(keep_a, after(got_a, keep_b))
    far_a = swap(near_a, "col", 2)
    near_b = add(keep_b, after(swap(send_b, "row", 1), near_a))
    far_b = swap(near_b, "row", 2)

    resid_a = residual_a(where, near_a, far_a, field_column, states_a, weight_rows)
    resid_a_other = swap(resid_a, "col", 1)
    far_states_b = swap(after(states_b, near_b), "col", 1)
    *hot, half_b, own = gradient_operands(
        where, states_a, states_b, far_states_b, couplings, states_a.shape[1] // side**2
    )
    keep_rb, send_rb = residual_b(where, near_b, after(far_b, resid_a, hot[0]), field_b, half_b, weight_column)
    send_rb_other = swap(send_rb, "row", 1)
    keep_rb_other = swap(keep_rb, "row", 1)
    resid_b = (keep_rb, keep_rb_other), (swap(send_rb, "col", 1), swap(send_rb_other, "col", 1))

    parts = gradient_parts(where, resid_a, resid_a_other, resid_b, hot, weight_rows, side)
    parts = middle_sums(where, send_parts(parts, sizes["col"], 0))
    mine, send = last_sums(where, send_parts(parts, sizes["col"], 1))
    return update(where, mine, swap(send, "col", 1), own)


def solution(mesh):
    placed = (
        P("seq", "row"),
        P("seq", "col"),
        P(None, "row"),
        P(None, "col"),
        P(None, None, "row", "col"),
        P("seq"),
    )
    return jax.shard_map(
        functools.partial(on_device, dict(mesh.shape)),
        mesh=mesh,
        in_specs=placed,
        out_specs=P(None, None, ("row", "seq"), "col"),
        check_vma=False,
    )
```
